32 devices in a mesh: grid: 8 (over z, x), freq: 4 (over y, core).
Axes of the slice: x: 2, y: 2, z: 4, core: 2. Of those that a mesh axis runs over, the one named last changes fastest.
Arguments:
- traces: bfloat16 [32, 8, 16, 2048], P(('grid', 'freq')), may hold values from -6 to 6
- bins: int32 [32, 8, 16], P(('grid', 'freq')), may hold values from 0 to 12287, as said below
- live: int32 [32, 8, 16], P(('grid', 'freq')), may hold values 0 or 1
- probe: float32 [64, 2, 24], replicated, may hold values from -0.5 to 0.5
Outputs:
- reconstructed: float32 [96, 16, 64, 512], P('grid', None, None, 'freq')
The draws below stay inside these ranges and needn't reach their ends.
Inputs may be any that keep to these rules, and one draw needn't show every extreme that they name: Within one destination tile the bins of all sources' slots are distinct; in each tile some slot names cell 0 and some slot names cell 12288 - 1.
All inputs are finite; a program needn't handle non-finite values. No bound on the sum of `live` on one device may be relied on, other than what follows from the above.
Results may differ from the reference program's by a relative error of at most 0.0052.
Values may be sent and summed in bfloat16 or wider, within the bound.
No kernel may reach another device: no remote copies, remote signals or barrier semaphores. Data moves between devices by JAX's collectives and lax.ppermute only.
A program may use at most 128 MiB of HBM per device.

```python
import math
import jax
import jax.numpy as jnp
from jax import lax

NT = 2048
FDEV = 64
FIRST = 8
RANK = 24
PX = 16
MY = 16
HX = 8
HY = 8
MARGIN = 2
SLOT = 16
OWNX = 12
NF = 256
NSRC = 32
CELLS = 12288
N_GRID = 8
N_FREQ = 4


def draw_bins(key, part):
    incoming = NSRC * SLOT

    def one_tile(patch_random_key):
        leading_seed = jax.random.fold_in(patch_random_key, 11)
        second_random_key = jax.random.fold_in(patch_random_key, 12)
        central_part = jax.random.permutation(leading_seed, CELLS - 2).astype(jnp.int32) + 1
        chosen = jnp.concatenate([jnp.array([CELLS - 1, 0], dtype=jnp.int32), central_part[:incoming - 2]])
        order = jax.random.permutation(second_random_key, incoming)
        return chosen[order].reshape(NSRC, SLOT)
    tile_keys = jax.vmap(lambda index: jax.random.fold_in(key, index))(jnp.arange(N_GRID, dtype=jnp.int32))
    per_tile = jax.vmap(one_tile)(tile_keys)
    return jnp.transpose(per_tile, (1, 0, 2)).astype(jnp.int32)


def plant(drawn, stream_key, smallest, top_value):
    longest = drawn.shape.index(max(drawn.shape))
    spots = []
    for shift in (0, 1):
        where = [jax.random.randint(jax.random.fold_in(stream_key, axis), (), 0, length) for axis, length in enumerate(drawn.shape)]
        where[longest] = (where[longest] + shift) % drawn.shape[longest]
        spots.append(tuple(where))
    return drawn.at[spots[0]].set(smallest).at[spots[1]].set(top_value)


def block_scale(rng, dims, split, low, largest):
    factor_of = 1.0
    for dim, shards_of in split:
        steps = jax.random.uniform(jax.random.fold_in(jax.random.fold_in(rng, 6), dim), (shards_of,), jnp.float32, low / len(split), largest / len(split))
        factor_of = factor_of * jnp.repeat(jnp.exp(steps), dims[dim] // shards_of).reshape((-1,) + (1,) * (len(dims) - 1 - dim))
    return factor_of


def scatter_about(own_key, shape, spread, most, cuts=(), kind=jnp.bfloat16):
    gain = block_scale(own_key, shape, cuts, -0.22, 0.18) if cuts else 1.0
    values = jax.random.normal(own_key, shape, jnp.float32) * spread * gain
    return jnp.minimum(jnp.maximum(values, -most), most).astype(kind)


def setup_inputs(seed: int = 0) -> dict:
    splits = jax.random.split(jax.random.key(seed), 5)
    return {
        "traces": scatter_about(splits[0], (NSRC, N_GRID, SLOT, NT), 1.0, 6.0, ((0, 32),)),
        "bins": draw_bins(jax.random.fold_in(splits[4], 71), 0),
        "live": plant((jax.random.randint(splits[2], (NSRC, N_GRID, SLOT), 0, 4) < 3).astype(jnp.int32), jax.random.fold_in(splits[2], 1), 0, 1),
        "probe": scatter_about(splits[3], (HX * HY, 2, RANK), (2 * HX * HY) ** -0.5, 0.5, (), jnp.float32),
    }


def spectral_table(recording_readings, fdev, band_count, first):
    clock_moments = jnp.arange(recording_readings, dtype=jnp.int32)[:, None]
    matrix_field = jnp.arange(2 * fdev * band_count, dtype=jnp.int32)[None, :]
    band_idx = matrix_field // (2 * fdev)
    half_idx = matrix_field // fdev % 2
    offset = matrix_field % fdev
    spectral_bin_number = first + band_idx * fdev + offset
    cycle_rotations = (clock_moments * spectral_bin_number % recording_readings).astype(jnp.float32) * (2.0 * math.pi / recording_readings)
    entries = jnp.where(half_idx == 0, jnp.cos(cycle_rotations), -jnp.sin(cycle_rotations)) / math.sqrt(recording_readings)
    return entries.astype(jnp.bfloat16)

def taper_weights(patch_x, margin):
    position = jnp.arange(patch_x, dtype=jnp.float32)
    ramp = jnp.minimum(position + 1.0, patch_x - position) / (2.0 * margin + 1.0)
    return jnp.minimum(ramp, 1.0)

def reduce_patch(window_record, probe):
    size_x, size_y, offsets, columns = window_record.shape
    fdev = columns // 2
    rank_count = probe.shape[-1]
    highest = lax.Precision.HIGHEST
    patch_rows = window_record.reshape(size_x * size_y, offsets, 2, fdev)
    sketch = jnp.einsum('mhcj,hcr->jmr', patch_rows, probe, precision=highest)
    gram = jnp.einsum('jmr,jms->jrs', sketch, sketch, precision=highest)
    identity = jnp.eye(rank_count, dtype=jnp.float32)
    diag_sum = lax.optimization_barrier(jnp.sum(gram * identity, axis=(1, 2)))
    gram = gram + (0.01 * diag_sum / rank_count + 1e-06)[:, None, None] * identity
    lower_factor = jnp.linalg.cholesky(gram)
    projected = jnp.einsum('jmr,mhcj->jrhc', sketch, patch_rows, precision=highest)
    projected = projected.reshape(fdev, rank_count, offsets * 2)
    inner = lax.linalg.triangular_solve(lower_factor, projected, left_side=True, lower=True)
    coeff = lax.linalg.triangular_solve(lower_factor, inner, left_side=True, lower=True, transpose_a=True)
    coeff = coeff.reshape(fdev, rank_count, offsets, 2)
    rebuilt = jnp.einsum('jmr,jrhc->mhcj', sketch, coeff, precision=highest)
    return rebuilt.reshape(size_x, size_y, offsets, columns)

def reference(traces, bins, live, probe):
    table = spectral_table(NT, FDEV, N_FREQ, FIRST)
    spectra = jnp.dot(traces.reshape(-1, NT).astype(jnp.float32), table.astype(jnp.float32), preferred_element_type=jnp.float32).astype(jnp.bfloat16)
    tile_ids = jnp.arange(N_GRID, dtype=jnp.int32)[None, :, None]
    flat_cells = jnp.where(live == 1, tile_ids * CELLS + bins, N_GRID * CELLS).astype(jnp.int32).reshape(-1)
    binned = jnp.zeros((N_GRID * CELLS, 2 * NF), jnp.bfloat16).at[flat_cells].set(spectra, mode='drop')
    binned = binned.reshape(N_GRID * OWNX, MY, HX * HY, 2 * NF)
    weights = taper_weights(PX, MARGIN)[:, None, None, None]

    def one_band(band_idx):
        band_data = lax.dynamic_slice_in_dim(binned, band_idx * 2 * FDEV, 2 * FDEV, 3)
        padded = jnp.pad(band_data, ((MARGIN, MARGIN), (0, 0), (0, 0), (0, 0)))

        def one_tile(block_number):
            window_record = lax.dynamic_slice_in_dim(padded, block_number * OWNX, PX, 0).astype(jnp.float32)
            return reduce_patch(window_record, probe) * weights
        pieces = lax.map(one_tile, jnp.arange(N_GRID, dtype=jnp.int32))
        core_part = pieces[:, MARGIN:PX - MARGIN]
        core_part = core_part.at[1:, :MARGIN].add(pieces[:-1, PX - MARGIN:])
        core_part = core_part.at[:-1, OWNX - MARGIN:].add(pieces[1:, :MARGIN])
        return core_part.reshape(N_GRID * OWNX, MY, HX * HY, 2 * FDEV)
    bands = lax.map(one_band, jnp.arange(N_FREQ, dtype=jnp.int32))
    return jnp.moveaxis(bands, 0, 3).reshape(N_GRID * OWNX, MY, HX * HY, 2 * NF)
```

```python
import functools
import math

import jax
import jax.numpy as jnp
from jax import lax
from jax.experimental import pallas as pl
from jax.experimental.pallas import tpu as pltpu
from jax.sharding import PartitionSpec as P

FDEV = 64
FIRST = 8
PX = 16
MY = 16
HC = 64
MARGIN = 2
OWNX = 12
RANK = 24
SPAN = 5
OWN_ROWS = OWNX * MY
RIM = MARGIN * MY
ROWS = PX * MY
COLS = 2 * FDEV
JG = 8
RP = 32
BLOCK_SRC = 32
DEAD = 255.0

f32 = jnp.float32
bf16 = jnp.bfloat16


def dot(a, b):
    return jnp.dot(a, b, preferred_element_type=f32)


def split(x):
    high = x.astype(bf16)
    return high, (x - high.astype(f32)).astype(bf16)


def iota(shape, dim):
    return lax.broadcasted_iota(jnp.int32, shape, dim)


def phase(times, columns, length, quarter):
    k = FIRST + columns // COLS * FDEV + columns % FDEV
    turns = ((times * k) & (length - 1)).astype(f32)
    angle = turns * (2.0 * math.pi / length)
    if quarter:
        angle = angle + (columns // FDEV % 2).astype(f32) * (0.5 * math.pi)
    return jnp.cos(angle), jnp.sin(angle)


def spectra_kernel(traces_ref, marks_ref, out_ref, table_ref):
    length, width = table_ref.shape
    tiles, bands = out_ref.shape[:2]
    slots = traces_ref.shape[0] // tiles
    coarse = length // 64
    column = iota((1, width), 1)
    col = lambda n: column + jnp.zeros((n, 1), jnp.int32)
    c1, s1 = phase(iota((coarse, width), 0) * 64, col(coarse), length, False)
    c2, s2 = phase(iota((8, width), 0) * 8, col(8), length, False)
    c3, s3 = phase(iota((8, width), 0), col(8), length, True)
    scale = 1.0 / math.sqrt(length)
    c3, s3 = c3 * scale, s3 * scale
    fine_c = jnp.concatenate([c2[i : i + 1] * c3 - s2[i : i + 1] * s3 for i in range(8)], 0)
    fine_s = jnp.concatenate([s2[i : i + 1] * c3 + c2[i : i + 1] * s3 for i in range(8)], 0)
    for i in range(coarse):
        block = c1[i : i + 1] * fine_c - s1[i : i + 1] * fine_s
        table_ref[64 * i : 64 * i + 64, :] = block.astype(bf16)
    spectra = dot(traces_ref[...], table_ref[...]).astype(bf16)
    nothing = jnp.zeros((slots, COLS), bf16)
    for band in range(bands):
        piece = spectra[:, band * COLS : (band + 1) * COLS]
        for tile in range(tiles):
            for t in range(SPAN):
                source = tile - 2 + t
                there = 0 <= source < tiles
                out_ref[tile, band, t * slots : (t + 1) * slots, :] = (
                    piece[source * slots : (source + 1) * slots] if there else nothing
                )
            out_ref[tile, band, SPAN * slots : SPAN * slots + 2, :] = marks_ref[tile]


def patch_kernel(
    tiles,
    slots,
    arrived_ref,
    probe_ref,
    out_ref,
    st_ref,
    pp_ref,
    own_ref,
    gram_ref,
    sem,
):
    sources = arrived_ref.shape[0]
    per = min(BLOCK_SRC, sources)
    n = per * slots
    chunks = sources // per
    nb = SPAN * chunks
    pl.run_scoped(
        functools.partial(project, slots, arrived_ref, probe_ref, st_ref, pp_ref, own_ref, gram_ref),
        pltpu.VMEM((nb, COLS, n), f32),
        pltpu.VMEM((nb, 2 * RANK, n), f32),
        pltpu.VMEM((nb, ROWS, n), bf16),
        pltpu.VMEM((nb, n, ROWS), bf16),
        pltpu.VMEM((nb, n, 3 * HC), bf16),
    )
    invert_grams(gram_ref)
    pl.run_scoped(
        functools.partial(write, tiles, own_ref, pp_ref, gram_ref, out_ref, sem),
        pltpu.VMEM((FDEV, OWN_ROWS, COLS), f32),
        pltpu.VMEM((OWN_ROWS, HC, COLS), f32),
    )


def over(chunks, body, carry):
    if chunks == 1:
        return body(0, carry)
    return lax.fori_loop(0, chunks, body, carry)


def project(
    slots,
    arrived_ref,
    probe_ref,
    st_ref,
    pp_ref,
    own_ref,
    gram_ref,
    vt_ref,
    wt_ref,
    ohm_ref,
    ohmt_ref,
    ohht_ref,
):
    sources = arrived_ref.shape[0]
    per = min(BLOCK_SRC, sources)
    n = per * slots
    chunks = sources // per
    group_of = (0, 0, 1, 2, 2)

    lane_src = (iota((per, n), 1) // slots == iota((per, n), 0)).astype(f32)
    for t in range(SPAN):

        def prepare(chunk, carry, t=t):
            b = t * chunks + chunk
            pick = (iota((COLS, n), 0) == t * slots + iota((COLS, n), 1) % slots).astype(f32).astype(bf16)
            marks = arrived_ref[pl.ds(chunk * per, per), SPAN * slots : SPAN * slots + 2, :].astype(f32)
            rows = []
            for i in range(2):
                spread = dot(marks[:, i, :].astype(bf16), pick)
                rows.append(jnp.sum(spread * lane_src, 0, keepdims=True))
            m, h = rows
            good = m < OWN_ROWS
            low, high = m < RIM, m >= OWN_ROWS - RIM
            if t == 0:
                inside = [good & high, None, None]
                place = jnp.where(good & high, m - (OWN_ROWS - RIM), DEAD + 1)
            elif t == 1:
                inside = [good, good & high, None]
                place = jnp.where(good, m + RIM, DEAD + 1)
            elif t == 2:
                inside = [good & low, good, good & high]
                place = jnp.where(good, m, DEAD + 1)
            elif t == 3:
                inside = [None, good & low, good]
                place = jnp.where(good, m, DEAD + 1)
            else:
                inside = [None, None, good & low]
                place = jnp.where(good & low, m + OWN_ROWS, DEAD + 1)
            offset = [
                jnp.full_like(h, -1.0) if ok is None else jnp.where(ok, h, -1.0) for ok in inside
            ]
            marks8 = jnp.concatenate([place] + offset + [h, h, h, h], 0)
            marks_t = marks8.T
            ohm_ref[b] = (iota((ROWS, n), 0).astype(f32) == place).astype(f32).astype(bf16)
            ohmt_ref[b] = (iota((n, ROWS), 1).astype(f32) == marks_t[:, 0:1]).astype(f32).astype(bf16)
            ohht_ref[b] = jnp.concatenate(
                [
                    (iota((n, HC), 1).astype(f32) == marks_t[:, 1 + p : 2 + p]).astype(f32)
                    for p in range(3)
                ],
                1,
            ).astype(bf16)
            ohh = (iota((HC, n), 0).astype(f32) == h).astype(f32).astype(bf16)
            p_high, p_low = split(probe_ref[...])
            wt_ref[b] = dot(p_high, ohh) + dot(p_low, ohh)
            values = arrived_ref[pl.ds(chunk * per, per), t * slots : (t + 1) * slots, :].reshape(n, COLS)
            vt_ref[b] = values.astype(f32).T
            return carry

        over(chunks, prepare, 0)

    st_ref[...] = jnp.zeros_like(st_ref)
    pp_ref[...] = jnp.zeros_like(pp_ref)
    lane = iota((RANK * JG, ROWS), 1)

    def step(g, carry):
        sketch = [None, None, None]
        for t in range(SPAN):

            def gather(chunk, total, t=t):
                b = t * chunks + chunk
                w = wt_ref[b]
                u = []
                for j in range(JG):
                    re = vt_ref[b, pl.ds(g * JG + j, 1), :]
                    im = vt_ref[b, pl.ds(FDEV + g * JG + j, 1), :]
                    u.append(w[:RANK] * re + w[RANK:] * im)
                part = dot(jnp.concatenate(u, 0).astype(bf16), ohmt_ref[b])
                return part if total is None else total + part

            k = group_of[t]
            first = None if chunks == 1 else jnp.zeros((RANK * JG, ROWS), f32)
            sketch[k] = over(chunks, gather, first if sketch[k] is None else sketch[k])
        left, own, right = sketch
        sk = [x.astype(bf16) for x in sketch]
        proj = None if chunks == 1 else jnp.zeros((2 * RANK * JG, 3 * HC), f32)
        for t in range(SPAN):

            def scatter(chunk, total, t=t):
                b = t * chunks + chunk
                at = dot(sk[group_of[t]], ohm_ref[b])
                z = []
                for c in range(2):
                    for j in range(JG):
                        v = vt_ref[b, pl.ds(c * FDEV + g * JG + j, 1), :]
                        z.append(at[j * RANK : (j + 1) * RANK] * v)
                part = dot(jnp.concatenate(z, 0).astype(bf16), ohht_ref[b])
                return part if total is None else total + part

            proj = over(chunks, scatter, proj)
        full_left = jnp.where(lane < ROWS - RIM, left, pltpu.roll(own, ROWS - RIM, 1))
        full_right = jnp.where(lane < ROWS - RIM, right, pltpu.roll(own, ROWS - OWN_ROWS, 1))
        full_own = jnp.where(
            lane < OWN_ROWS,
            own,
            jnp.where(lane < OWN_ROWS + RIM, left, pltpu.roll(right, ROWS - RIM, 1)),
        )
        half = RANK * JG
        re, im = proj[:half], proj[half:]
        lo = iota((half, COLS), 1) < HC
        parts = [
            jnp.where(lo, re[:, :COLS], pltpu.roll(im[:, :COLS], HC, 1)),
            jnp.where(lo, pltpu.roll(re[:, :COLS], HC, 1), im[:, :COLS]),
            jnp.where(
                lo,
                jnp.concatenate([re[:, COLS:], re[:, COLS:]], 1),
                jnp.concatenate([im[:, COLS:], im[:, COLS:]], 1),
            ),
        ]
        for p, whole in enumerate((full_left, full_own, full_right)):
            st_ref[p, :, :RANK, :] = whole.reshape(JG, RANK, ROWS)
            pp_ref[p, pl.ds(g * JG, JG), :RANK, :] = parts[p].reshape(JG, RANK, COLS)
            pad = st_ref[p].reshape(JG * RP, ROWS).astype(bf16)
            if p == 1:
                own_ref[g] = st_ref[p].reshape(JG * RP, ROWS).T[:OWN_ROWS].astype(bf16)
            gram = lax.dot_general(pad, pad, (((1,), (1,)), ((), ())), preferred_element_type=f32)
            for q2 in range(2):
                lanes = iota((RANK, 4 * RP), 1) // RP
                acc = jnp.zeros((RANK, 4 * RP), f32)
                for q in range(4):
                    at = (q2 * 4 + q) * RP
                    piece = gram[at : at + RANK, q2 * 4 * RP : (q2 + 1) * 4 * RP]
                    acc = jnp.where(lanes == q, piece, acc)
                gram_ref[p, 2 * g + q2] = acc
        return carry

    lax.fori_loop(0, FDEV // JG, step, 0)


def invert_grams(gram_ref):
    count = FDEV // 4
    batch = 8
    wide = 4 * RP
    lane3 = iota((batch, RANK, wide), 2) % RP
    row3 = iota((batch, RANK, wide), 1)
    lane1 = iota((batch, 1, wide), 2) % RP
    base = iota((batch * RANK, wide), 1) // RP * RP
    same = (iota((wide, wide), 0) // RP == iota((wide, wide), 1) // RP).astype(f32)

    def invert(i, carry):
        p, c = i // (count // batch), i % (count // batch)
        a = gram_ref[p, pl.ds(c * batch, batch)]
        diag = jnp.sum(jnp.where(lane3 == row3, a, 0.0), 1)
        trace = jnp.dot(
            diag, same, preferred_element_type=f32, precision=lax.Precision.HIGHEST
        )
        ridge = 0.01 * trace / RANK + 1e-06
        a = a + jnp.where(lane3 == row3, ridge[:, None, :], 0.0)
        for k in range(RANK):
            flat = a.reshape(batch * RANK, wide)
            column = jnp.take_along_axis(flat, base + k, axis=1).reshape(batch, RANK, wide)
            scale = 1.0 / column[:, k : k + 1]
            pivot = jnp.where(lane1 == k, scale, a[:, k : k + 1] * scale)
            rest = jnp.where(lane3 == k, 0.0, a) - column * pivot
            a = jnp.where(row3 == k, pivot, rest)
        gram_ref[p, pl.ds(c * batch, batch)] = a
        return carry

    lax.fori_loop(0, 3 * count // batch, invert, 0)


def write(tiles, own_ref, pp_ref, gram_ref, out_ref, sem, freq_ref, cells_ref):
    count = FDEV // 4
    wide = 4 * RP
    here = lax.axis_index("grid")
    has_left = (here > 0).astype(f32)
    has_right = (here < tiles - 1).astype(f32)
    edge = iota((RIM, 1), 0) < MY
    taper_first = jnp.where(edge, 0.6, 0.8)
    taper_last = jnp.where(edge, 0.8, 0.6)
    left_w = jnp.where(edge, 0.4, 0.2) * has_left
    right_w = jnp.where(edge, 0.2, 0.4) * has_right

    def rebuild(i, carry):
        rows = own_ref[i // 2, :, pl.ds(pl.multiple_of(i % 2 * wide, wide), wide)]
        weights = []
        for p in range(3):
            inverse = gram_ref[p, i]
            lanes = iota((RANK, wide), 1) // RP
            zero = jnp.zeros((RP - RANK, wide), f32)
            diag = []
            for q in range(4):
                diag += [jnp.where(lanes == q, inverse, 0.0), zero]
            b_high, b_low = split(jnp.concatenate(diag, 0))
            p_high, p_low = split(pp_ref[p, pl.ds(i * 4, 4)].reshape(wide, COLS))
            coeff = dot(b_high, p_high) + dot(b_high, p_low) + dot(b_low, p_high)
            weights.append(coeff)
        quarter = iota((wide, COLS), 0) // RP
        for a in range(2):
            w = [
                jnp.concatenate([jnp.where(quarter == 2 * a + e, x, 0.0) for e in range(2)], 1).astype(bf16)
                for x in weights
            ]
            mid = dot(rows, w[1])
            first = mid[:RIM] * taper_first + dot(rows[:RIM], w[0]) * left_w
            last = mid[OWN_ROWS - RIM :] * taper_last + dot(rows[OWN_ROWS - RIM :], w[2]) * right_w
            full = jnp.concatenate([first, mid[RIM : OWN_ROWS - RIM], last], 0)
            for e in range(2):
                freq_ref[i * 4 + 2 * a + e] = full[:, e * COLS : (e + 1) * COLS]
        return carry

    lax.fori_loop(0, count, rebuild, 0)

    unroll = 4
    half_lane = iota((HC, COLS), 1) < FDEV

    def turn(i, carry):
        for q in range(unroll):
            m = (i * unroll + q) * 2
            both = jnp.concatenate([freq_ref[:, m, :], freq_ref[:, m + 1, :]], 0)
            flip = both.T
            re, im = flip[:HC], flip[HC:]
            cells_ref[m] = jnp.where(half_lane, re, pltpu.roll(im, FDEV, 1))
            cells_ref[m + 1] = jnp.where(half_lane, pltpu.roll(re, FDEV, 1), im)
        return carry

    pieces = 6
    size = OWN_ROWS // pieces
    copies = []
    for k in range(pieces):
        per_piece = size // (2 * unroll)
        lax.fori_loop(k * per_piece, (k + 1) * per_piece, turn, 0)
        copy = pltpu.make_async_copy(
            cells_ref.at[pl.ds(k * size, size)], out_ref.at[pl.ds(k * size, size)], sem.at[k]
        )
        copy.start()
        copies.append(copy)
    for copy in copies:
        copy.wait()


def per_device(traces, bins, live, probe):
    tiles = lax.axis_size("grid")
    bands = lax.axis_size("freq")
    slots, length = traces.shape[2:]
    sources = tiles * bands
    used = SPAN * slots

    on = live[0] == 1
    mark = jnp.stack(
        [jnp.where(on, bins[0] // HC, int(DEAD)), jnp.where(on, bins[0] % HC, 0)], 1
    ).astype(bf16)
    mark = jnp.pad(mark, ((2, 2), (0, 0), (0, 0)), constant_values=DEAD)
    marks = jnp.concatenate([mark[t : t + tiles] for t in range(SPAN)], 2)
    marks = jnp.pad(marks, ((0, 0), (0, 0), (0, COLS - used)))

    vmem = pl.BlockSpec(memory_space=pltpu.VMEM)
    sent = pl.pallas_call(
        spectra_kernel,
        out_shape=jax.ShapeDtypeStruct((tiles, bands, used + 2, COLS), bf16),
        in_specs=[vmem, vmem],
        out_specs=vmem,
        scratch_shapes=[pltpu.VMEM((length, COLS * bands), bf16)],
        compiler_params=pltpu.CompilerParams(vmem_limit_bytes=48 * 2**20),
        name="spectra",
    )(traces.reshape(tiles * slots, length), marks)

    arrived = lax.all_to_all(
        sent.reshape(sources, used + 2, COLS), ("grid", "freq"), 0, 0, tiled=True
    )

    out = pl.pallas_call(
        functools.partial(patch_kernel, tiles, slots),
        out_shape=jax.ShapeDtypeStruct((OWN_ROWS, HC, COLS), f32),
        in_specs=[vmem, vmem],
        out_specs=pl.BlockSpec(memory_space=pl.ANY),
        scratch_shapes=[
            pltpu.VMEM((3, JG, RP, ROWS), f32),
            pltpu.VMEM((3, FDEV, RP, COLS), f32),
            pltpu.VMEM((FDEV // JG, OWN_ROWS, JG * RP), bf16),
            pltpu.VMEM((3, FDEV // 4, RANK, 4 * RP), f32),
            pltpu.SemaphoreType.DMA((6,)),
        ],
        compiler_params=pltpu.CompilerParams(vmem_limit_bytes=60 * 2**20),
        name="patches",
    )(arrived, jnp.transpose(probe, (1, 2, 0)).reshape(2 * RANK, HC))
    return out.reshape(OWNX, MY, HC, COLS)


def solution(mesh):
    placed = (
        P(("grid", "freq"), None, None, None),
        P(("grid", "freq"), None, None),
        P(("grid", "freq"), None, None),
        P(),
    )
    return jax.shard_map(
        per_device,
        mesh=mesh,
        in_specs=placed,
        out_specs=P("grid", None, None, "freq"),
        check_vma=False,
    )
```

```python
import functools
import math

import jax
import jax.numpy as jnp
from jax import lax
from jax.experimental import pallas as pl
from jax.experimental.pallas import tpu as pltpu
from jax.sharding import PartitionSpec as P

FDEV = 64
FIRST = 8
PX = 16
MY = 16
HC = 64
MARGIN = 2
OWNX = 12
RANK = 24
SPAN = 5
OWN_ROWS = OWNX * MY
RIM = MARGIN * MY
ROWS = PX * MY
COLS = 2 * FDEV
JG = 8
RP = 32
BLOCK_SRC = 32
DEAD = 255.0

f32 = jnp.float32
bf16 = jnp.bfloat16


def dot(a, b):
    return jnp.dot(a, b, preferred_element_type=f32)


def split(x):
    high = x.astype(bf16)
    return high, (x - high.astype(f32)).astype(bf16)


def iota(shape, dim):
    return lax.broadcasted_iota(jnp.int32, shape, dim)


def phase(times, columns, length, quarter):
    k = FIRST + columns // COLS * FDEV + columns % FDEV
    turns = ((times * k) & (length - 1)).astype(f32)
    angle = turns * (2.0 * math.pi / length)
    if quarter:
        angle = angle + (columns // FDEV % 2).astype(f32) * (0.5 * math.pi)
    return jnp.cos(angle), jnp.sin(angle)


def spectra_kernel(traces_ref, marks_ref, out_ref, table_ref):
    length, width = table_ref.shape
    tiles, bands = out_ref.shape[:2]
    slots = traces_ref.shape[0] // tiles
    coarse = length // 64
    column = iota((1, width), 1)
    col = lambda n: column + jnp.zeros((n, 1), jnp.int32)
    c1, s1 = phase(iota((coarse, width), 0) * 64, col(coarse), length, False)
    c2, s2 = phase(iota((8, width), 0) * 8, col(8), length, False)
    c3, s3 = phase(iota((8, width), 0), col(8), length, True)
    scale = 1.0 / math.sqrt(length)
    c3, s3 = c3 * scale, s3 * scale
    fine_c = jnp.concatenate([c2[i : i + 1] * c3 - s2[i : i + 1] * s3 for i in range(8)], 0)
    fine_s = jnp.concatenate([s2[i : i + 1] * c3 + c2[i : i + 1] * s3 for i in range(8)], 0)
    for i in range(coarse):
        block = c1[i : i + 1] * fine_c - s1[i : i + 1] * fine_s
        table_ref[64 * i : 64 * i + 64, :] = block.astype(bf16)
    spectra = dot(traces_ref[...], table_ref[...]).astype(bf16)
    nothing = jnp.zeros((slots, COLS), bf16)
    for band in range(bands):
        piece = spectra[:, band * COLS : (band + 1) * COLS]
        for tile in range(tiles):
            for t in range(SPAN):
                source = tile - 2 + t
                there = 0 <= source < tiles
                out_ref[tile, band, t * slots : (t + 1) * slots, :] = (
                    piece[source * slots : (source + 1) * slots] if there else nothing
                )
            out_ref[tile, band, SPAN * slots : SPAN * slots + 2, :] = marks_ref[tile]


def patch_kernel(
    tiles,
    slots,
    arrived_ref,
    probe_ref,
    out_ref,
    st_ref,
    pp_ref,
    own_ref,
    gram_ref,
    sem,
):
    sources = arrived_ref.shape[0]
    per = min(BLOCK_SRC, sources)
    n = per * slots
    chunks = sources // per
    side = chunks + rim_blocks(chunks, n)
    nb = chunks + 2 * side
    pl.run_scoped(
        functools.partial(project, slots, arrived_ref, probe_ref, st_ref, pp_ref, own_ref, gram_ref),
        pltpu.VMEM((nb, COLS, n), f32),
        pltpu.VMEM((nb, 2 * RANK, n), f32),
        pltpu.VMEM((nb, ROWS, n), bf16),
        pltpu.VMEM((nb, n, ROWS), bf16),
        pltpu.VMEM((nb, n, 3 * HC), bf16),
        pltpu.VMEM((SPAN * chunks, 1, n), f32),
        pltpu.VMEM((SPAN * chunks, 8, n), f32),
    )
    invert_grams(gram_ref)
    pl.run_scoped(
        functools.partial(write, tiles, own_ref, pp_ref, gram_ref, out_ref, sem),
        pltpu.VMEM((FDEV, OWN_ROWS, COLS), f32),
        pltpu.VMEM((OWN_ROWS, HC, COLS), f32),
    )


def rim_blocks(chunks, n):
    return (min(RIM * HC, chunks * n) + n - 1) // n


def over(chunks, body, carry):
    if chunks == 1:
        return body(0, carry)
    return lax.fori_loop(0, chunks, body, carry)


def project(
    slots,
    arrived_ref,
    probe_ref,
    st_ref,
    pp_ref,
    own_ref,
    gram_ref,
    vt_ref,
    wt_ref,
    ohm_ref,
    ohmt_ref,
    ohht_ref,
    rank_ref,
    fact_ref,
):
    sources = arrived_ref.shape[0]
    per = min(BLOCK_SRC, sources)
    n = per * slots
    chunks = sources // per
    members = ((0, 1), (2,), (3, 4))
    side = chunks + rim_blocks(chunks, n)
    first = (0, side, side + chunks)

    lane_src = (iota((per, n), 1) // slots == iota((per, n), 0)).astype(f32)
    before = (iota((n, n), 0) < iota((n, n), 1)).astype(f32).astype(bf16)

    def locate(chunk, totals):
        totals = list(totals)
        marks = arrived_ref[pl.ds(chunk * per, per), SPAN * slots : SPAN * slots + 2, :].astype(f32)
        facts, used = [], []
        for t in range(SPAN):
            pick = (iota((COLS, n), 0) == t * slots + iota((COLS, n), 1) % slots).astype(f32)
            pick = pick.astype(bf16)
            rows = []
            for i in range(2):
                spread = dot(marks[:, i, :].astype(bf16), pick)
                rows.append(jnp.sum(spread * lane_src, 0, keepdims=True))
            m, h = rows
            good = m < OWN_ROWS
            low, high = m < RIM, good & (m >= OWN_ROWS - RIM)
            keep = (high, good, good, good, low)[t]
            shift = (RIM - OWN_ROWS, RIM, 0, 0, OWN_ROWS)[t]
            inside = (
                (high, None, None),
                (good, high, None),
                (low, good, high),
                (None, low, good),
                (None, None, low),
            )[t]
            fact = [jnp.where(keep, m + shift + 1.0, 0.0), jnp.where(keep, h + 1.0, 0.0)]
            for ok in inside:
                fact.append(jnp.zeros_like(h) if ok is None else jnp.where(ok, h + 1.0, 0.0))
            facts.append(jnp.concatenate(fact + [jnp.zeros((3, n), f32)], 0))
            used.append(keep.astype(f32))
        use = jnp.concatenate(used + [jnp.zeros((8 - SPAN, n), f32)], 0)
        ranks = dot(use.astype(bf16), before)
        sums = jnp.sum(use, 1, keepdims=True)
        for k in range(3):
            for t in members[k]:
                rank = ranks[t : t + 1] + totals[k]
                rank_ref[t * chunks + chunk] = jnp.where(use[t : t + 1] > 0.5, rank, -1.0)
                fact_ref[t * chunks + chunk] = facts[t]
                totals[k] = totals[k] + sums[t : t + 1]
        return tuple(totals)

    zero = jnp.zeros((1, 1), f32)
    totals = over(chunks, locate, (zero, zero, zero))
    counts = [jnp.max(x).astype(jnp.int32) for x in totals]
    filled = [(c + (n - 1)) // n for c in counts]

    p_high, p_low = split(probe_ref[...])

    def pack(k, q):
        def gather(chunk, total, t):
            b = t * chunks + chunk
            wanted = iota((n, n), 0).astype(f32) + (q * n).astype(f32)
            chosen = (wanted == rank_ref[b]).astype(f32).astype(bf16)
            values = arrived_ref[pl.ds(chunk * per, per), t * slots : (t + 1) * slots, :]
            fact = jnp.concatenate([fact_ref[b], jnp.zeros((COLS - 8, n), f32)], 0).T
            both = jnp.concatenate([values.reshape(n, COLS), fact.astype(bf16)], 1)
            part = dot(chosen, both)
            return part if total is None else total + part

        total = None if chunks == 1 else jnp.zeros((n, 2 * COLS), f32)
        for t in members[k]:
            total = over(chunks, functools.partial(gather, t=t), total)
        flip = total.T
        b = first[k] + q
        vt_ref[b] = flip[:COLS]
        row, h = flip[COLS : COLS + 1] - 1.0, flip[COLS + 1 : COLS + 2] - 1.0
        column = total[:, COLS : COLS + 8] - 1.0
        ohm_ref[b] = (iota((ROWS, n), 0).astype(f32) == row).astype(f32).astype(bf16)
        ohmt_ref[b] = (iota((n, ROWS), 1).astype(f32) == column[:, 0:1]).astype(f32).astype(bf16)
        ohht_ref[b] = jnp.concatenate(
            [
                (iota((n, HC), 1).astype(f32) == column[:, 2 + p : 3 + p]).astype(f32)
                for p in range(3)
            ],
            1,
        ).astype(bf16)
        ohh = (iota((HC, n), 0).astype(f32) == h).astype(f32).astype(bf16)
        wt_ref[b] = dot(p_high, ohh) + dot(p_low, ohh)

    for k in range(3):
        pack(k, jnp.int32(0))

        def more(q, carry, k=k):
            pack(k, q)
            return carry

        lax.fori_loop(1, filled[k], more, 0)

    st_ref[:, :, RANK:, :] = jnp.zeros((3, JG, RP - RANK, ROWS), f32)
    pp_ref[:, :, RANK:, :] = jnp.zeros((3, FDEV, RP - RANK, COLS), f32)
    lane = iota((RANK * JG, ROWS), 1)

    def step(g, carry, short):
        def sketch_of(b):
            w = wt_ref[b]
            u = []
            for j in range(JG):
                re = vt_ref[b, pl.ds(g * JG + j, 1), :]
                im = vt_ref[b, pl.ds(FDEV + g * JG + j, 1), :]
                u.append(w[:RANK] * re + w[RANK:] * im)
            return dot(jnp.concatenate(u, 0).astype(bf16), ohmt_ref[b])

        def project_of(b, rows):
            at = dot(rows, ohm_ref[b])
            z = []
            for c in range(2):
                for j in range(JG):
                    v = vt_ref[b, pl.ds(c * FDEV + g * JG + j, 1), :]
                    z.append(at[j * RANK : (j + 1) * RANK] * v)
            return dot(jnp.concatenate(z, 0).astype(bf16), ohht_ref[b])

        sketch = [sketch_of(first[k]) for k in range(3)]
        if not short:
            for k in range(3):
                sketch[k] = lax.fori_loop(
                    1, filled[k], lambda q, x, k=k: x + sketch_of(first[k] + q), sketch[k]
                )
        left, own, right = sketch
        sk = [x.astype(bf16) for x in sketch]
        proj = sum(project_of(first[k], sk[k]) for k in range(3))
        if not short:
            for k in range(3):
                proj = lax.fori_loop(
                    1, filled[k], lambda q, x, k=k: x + project_of(first[k] + q, sk[k]), proj
                )
        full_left = jnp.where(lane < ROWS - RIM, left, pltpu.roll(own, ROWS - RIM, 1))
        full_right = jnp.where(lane < ROWS - RIM, right, pltpu.roll(own, ROWS - OWN_ROWS, 1))
        full_own = jnp.where(
            lane < OWN_ROWS,
            own,
            jnp.where(lane < OWN_ROWS + RIM, left, pltpu.roll(right, ROWS - RIM, 1)),
        )
        half = RANK * JG
        re, im = proj[:half], proj[half:]
        lo = iota((half, COLS), 1) < HC
        parts = [
            jnp.where(lo, re[:, :COLS], pltpu.roll(im[:, :COLS], HC, 1)),
            jnp.where(lo, pltpu.roll(re[:, :COLS], HC, 1), im[:, :COLS]),
            jnp.where(
                lo,
                jnp.concatenate([re[:, COLS:], re[:, COLS:]], 1),
                jnp.concatenate([im[:, COLS:], im[:, COLS:]], 1),
            ),
        ]
        for p, whole in enumerate((full_left, full_own, full_right)):
            st_ref[p, :, :RANK, :] = whole.reshape(JG, RANK, ROWS)
            pp_ref[p, pl.ds(g * JG, JG), :RANK, :] = parts[p].reshape(JG, RANK, COLS)
            pad = st_ref[p].reshape(JG * RP, ROWS).astype(bf16)
            if p == 1:
                own_ref[g] = st_ref[p].reshape(JG * RP, ROWS).T[:OWN_ROWS].astype(bf16)
            gram = lax.dot_general(pad, pad, (((1,), (1,)), ((), ())), preferred_element_type=f32)
            for q2 in range(2):
                lanes = iota((RANK, 4 * RP), 1) // RP
                acc = jnp.zeros((RANK, 4 * RP), f32)
                for q in range(4):
                    at = (q2 * 4 + q) * RP
                    piece = gram[at : at + RANK, q2 * 4 * RP : (q2 + 1) * 4 * RP]
                    acc = jnp.where(lanes == q, piece, acc)
                gram_ref[p * (FDEV // 4) + 2 * g + q2] = acc
        return carry

    one_block = jnp.maximum(jnp.maximum(filled[0], filled[1]), filled[2]) <= 1

    @pl.when(one_block)
    def _():
        lax.fori_loop(0, FDEV // JG, functools.partial(step, short=True), 0)

    @pl.when(jnp.logical_not(one_block))
    def _():
        lax.fori_loop(0, FDEV // JG, functools.partial(step, short=False), 0)


def invert_grams(gram_ref):
    count = 3 * FDEV // 4
    batch = 48
    wide = 4 * RP
    lane3 = iota((batch, RANK, wide), 2) % RP
    row3 = iota((batch, RANK, wide), 1)
    lane1 = iota((batch, 1, wide), 2) % RP
    base = iota((batch * RANK, wide), 1) // RP * RP
    same = (iota((wide, wide), 0) // RP == iota((wide, wide), 1) // RP).astype(f32)

    def invert(i, carry):
        a = gram_ref[pl.ds(i * batch, batch)]
        diag = jnp.sum(jnp.where(lane3 == row3, a, 0.0), 1)
        trace = jnp.dot(
            diag, same, preferred_element_type=f32, precision=lax.Precision.HIGHEST
        )
        ridge = 0.01 * trace / RANK + 1e-06
        a = a + jnp.where(lane3 == row3, ridge[:, None, :], 0.0)
        for k in range(0, RANK, 2):
            flat = a.reshape(batch * RANK, wide)
            c0 = jnp.take_along_axis(flat, base + k, axis=1).reshape(batch, RANK, wide)
            c1 = jnp.take_along_axis(flat, base + k + 1, axis=1).reshape(batch, RANK, wide)
            x, y, z = c0[:, k : k + 1], c1[:, k : k + 1], c1[:, k + 1 : k + 2]
            scale = 1.0 / (x * z - y * y)
            x, y, z = z * scale, -y * scale, x * scale
            r0, r1 = a[:, k : k + 1], a[:, k + 1 : k + 2]
            n0 = jnp.where(lane1 == k, x, jnp.where(lane1 == k + 1, y, x * r0 + y * r1))
            n1 = jnp.where(lane1 == k, y, jnp.where(lane1 == k + 1, z, y * r0 + z * r1))
            a = jnp.where(lane3 // 2 == k // 2, 0.0, a) - c0 * n0 - c1 * n1
            a = jnp.where(row3 == k, n0, jnp.where(row3 == k + 1, n1, a))
        gram_ref[pl.ds(i * batch, batch)] = a
        return carry

    lax.fori_loop(0, count // batch, invert, 0)


def write(tiles, own_ref, pp_ref, gram_ref, out_ref, sem, freq_ref, cells_ref):
    count = FDEV // 4
    wide = 4 * RP
    here = lax.axis_index("grid")
    has_left = (here > 0).astype(f32)
    has_right = (here < tiles - 1).astype(f32)
    edge = iota((RIM, 1), 0) < MY
    taper_first = jnp.where(edge, 0.6, 0.8)
    taper_last = jnp.where(edge, 0.8, 0.6)
    left_w = jnp.where(edge, 0.4, 0.2) * has_left
    right_w = jnp.where(edge, 0.2, 0.4) * has_right

    def rebuild(i, carry):
        rows = own_ref[i // 2, :, pl.ds(pl.multiple_of(i % 2 * wide, wide), wide)]
        weights = []
        for p in range(3):
            inverse = gram_ref[p * count + i]
            lanes = iota((RANK, wide), 1) // RP
            zero = jnp.zeros((RP - RANK, wide), f32)
            diag = []
            for q in range(4):
                diag += [jnp.where(lanes == q, inverse, 0.0), zero]
            b_high, b_low = split(jnp.concatenate(diag, 0))
            p_high, p_low = split(pp_ref[p, pl.ds(i * 4, 4)].reshape(wide, COLS))
            coeff = dot(b_high, p_high) + dot(b_high, p_low) + dot(b_low, p_high)
            weights.append(coeff)
        quarter = iota((wide, COLS), 0) // RP
        for a in range(2):
            w = [
                jnp.concatenate([jnp.where(quarter == 2 * a + e, x, 0.0) for e in range(2)], 1).astype(bf16)
                for x in weights
            ]
            mid = dot(rows, w[1])
            first = mid[:RIM] * taper_first + dot(rows[:RIM], w[0]) * left_w
            last = mid[OWN_ROWS - RIM :] * taper_last + dot(rows[OWN_ROWS - RIM :], w[2]) * right_w
            full = jnp.concatenate([first, mid[RIM : OWN_ROWS - RIM], last], 0)
            for e in range(2):
                freq_ref[i * 4 + 2 * a + e] = full[:, e * COLS : (e + 1) * COLS]
        return carry

    lax.fori_loop(0, count, rebuild, 0)

    unroll = 4
    half_lane = iota((HC, COLS), 1) < FDEV

    def turn(i, carry):
        for q in range(unroll):
            m = (i * unroll + q) * 2
            both = jnp.concatenate([freq_ref[:, m, :], freq_ref[:, m + 1, :]], 0)
            flip = both.T
            re, im = flip[:HC], flip[HC:]
            cells_ref[m] = jnp.where(half_lane, re, pltpu.roll(im, FDEV, 1))
            cells_ref[m + 1] = jnp.where(half_lane, pltpu.roll(re, FDEV, 1), im)
        return carry

    pieces = 6
    size = OWN_ROWS // pieces
    copies = []
    for k in range(pieces):
        per_piece = size // (2 * unroll)
        lax.fori_loop(k * per_piece, (k + 1) * per_piece, turn, 0)
        copy = pltpu.make_async_copy(
            cells_ref.at[pl.ds(k * size, size)], out_ref.at[pl.ds(k * size, size)], sem.at[k]
        )
        copy.start()
        copies.append(copy)
    for copy in copies:
        copy.wait()


def patches(arrived, probe, tiles, slots):
    return pl.pallas_call(
        functools.partial(patch_kernel, tiles, slots),
        out_shape=jax.ShapeDtypeStruct((OWN_ROWS, HC, COLS), f32),
        in_specs=[pl.BlockSpec(memory_space=pltpu.VMEM)] * 2,
        out_specs=pl.BlockSpec(memory_space=pl.ANY),
        scratch_shapes=[
            pltpu.VMEM((3, JG, RP, ROWS), f32),
            pltpu.VMEM((3, FDEV, RP, COLS), f32),
            pltpu.VMEM((FDEV // JG, OWN_ROWS, JG * RP), bf16),
            pltpu.VMEM((3 * FDEV // 4, RANK, 4 * RP), f32),
            pltpu.SemaphoreType.DMA((6,)),
        ],
        compiler_params=pltpu.CompilerParams(vmem_limit_bytes=60 * 2**20),
        name="patches",
    )(arrived, probe)


def per_device(traces, bins, live, probe):
    tiles = lax.axis_size("grid")
    bands = lax.axis_size("freq")
    slots, length = traces.shape[2:]
    sources = tiles * bands
    used = SPAN * slots

    on = live[0] == 1
    mark = jnp.stack(
        [jnp.where(on, bins[0] // HC, int(DEAD)), jnp.where(on, bins[0] % HC, 0)], 1
    ).astype(bf16)
    mark = jnp.pad(mark, ((2, 2), (0, 0), (0, 0)), constant_values=DEAD)
    marks = jnp.concatenate([mark[t : t + tiles] for t in range(SPAN)], 2)
    marks = jnp.pad(marks, ((0, 0), (0, 0), (0, COLS - used)))

    vmem = pl.BlockSpec(memory_space=pltpu.VMEM)
    sent = pl.pallas_call(
        spectra_kernel,
        out_shape=jax.ShapeDtypeStruct((tiles, bands, used + 2, COLS), bf16),
        in_specs=[vmem, vmem],
        out_specs=vmem,
        scratch_shapes=[pltpu.VMEM((length, COLS * bands), bf16)],
        compiler_params=pltpu.CompilerParams(vmem_limit_bytes=48 * 2**20),
        name="spectra",
    )(traces.reshape(tiles * slots, length), marks)

    arrived = lax.all_to_all(
        sent.reshape(sources, used + 2, COLS), ("grid", "freq"), 0, 0, tiled=True
    )

    out = patches(
        arrived, jnp.transpose(probe, (1, 2, 0)).reshape(2 * RANK, HC), tiles, slots
    )
    return out.reshape(OWNX, MY, HC, COLS)


def solution(mesh):
    placed = (
        P(("grid", "freq"), None, None, None),
        P(("grid", "freq"), None, None),
        P(("grid", "freq"), None, None),
        P(),
    )
    return jax.shard_map(
        per_device,
        mesh=mesh,
        in_specs=placed,
        out_specs=P("grid", None, None, "freq"),
        check_vma=False,
    )
```

```python
import functools
import math

import jax
import jax.numpy as jnp
from jax import lax
from jax.experimental import pallas as pl
from jax.experimental.pallas import tpu as pltpu
from jax.sharding import PartitionSpec as P

FDEV = 64
FIRST = 8
PX = 16
MY = 16
HC = 64
MARGIN = 2
OWNX = 12
RANK = 24
SPAN = 5
OWN_ROWS = OWNX * MY
RIM = MARGIN * MY
ROWS = PX * MY
PAIRS = OWN_ROWS // 2
COLS = 2 * FDEV
JG = 8
RP = 32
BLOCK_SRC = 32
DEAD = 255.0

f32 = jnp.float32
bf16 = jnp.bfloat16


def dot(a, b):
    return jnp.dot(a, b, preferred_element_type=f32)


def split(x):
    high = x.astype(bf16)
    return high, (x - high.astype(f32)).astype(bf16)


def iota(shape, dim):
    return lax.broadcasted_iota(jnp.int32, shape, dim)


def phase(times, columns, length, quarter):
    k = FIRST + columns // COLS * FDEV + columns % FDEV
    turns = ((times * k) & (length - 1)).astype(f32)
    angle = turns * (2.0 * math.pi / length)
    if quarter:
        angle = angle + (columns // FDEV % 2).astype(f32) * (0.5 * math.pi)
    return jnp.cos(angle), jnp.sin(angle)


def marks_of(bins_ref, live_ref):
    tiles, slots = bins_ref.shape
    on = live_ref[...] == 1
    both = jnp.concatenate(
        [
            jnp.where(on, bins_ref[...] // HC, int(DEAD)),
            jnp.where(on, bins_ref[...] % HC, 0),
        ],
        0,
    )
    lanes = iota((slots, SPAN * COLS), 1)
    put = (lanes % COLS == lanes // COLS * slots + iota((slots, SPAN * COLS), 0)).astype(f32)
    placed = dot(both.astype(f32).astype(bf16), put.astype(bf16))
    tile, lane = iota((tiles, COLS), 0), iota((tiles, COLS), 1)
    marks = []
    for i, other in enumerate((DEAD, 0.0)):
        mark = jnp.full((tiles, COLS), other, f32)
        for t in range(SPAN):
            moved = placed[i * tiles : (i + 1) * tiles, t * COLS : (t + 1) * COLS]
            if t != 2:
                moved = pltpu.roll(moved, (2 - t) % tiles, 0)
            there = (tile + (t - 2) >= 0) & (tile + (t - 2) < tiles) & (lane // slots == t)
            mark = jnp.where(there, moved, mark)
        marks.append(mark.astype(bf16))
    return marks


def spectra_kernel(
    traces_ref, bins_ref, live_ref, out_ref, table_ref, held_ref, bins_held, live_held, sem
):
    length, width = table_ref.shape
    tiles, bands = out_ref.shape[:2]
    slots = bins_ref.shape[1]
    moves = ((bins_ref, bins_held), (live_ref, live_held), (traces_ref, held_ref))
    copies = [pltpu.make_async_copy(a, b, sem.at[i]) for i, (a, b) in enumerate(moves)]
    for copy in copies:
        copy.start()
    coarse = length // 64
    column = iota((1, width), 1)
    col = lambda n: column + jnp.zeros((n, 1), jnp.int32)
    c1, s1 = phase(iota((coarse, width), 0) * 64, col(coarse), length, False)
    c2, s2 = phase(iota((8, width), 0) * 8, col(8), length, False)
    c3, s3 = phase(iota((8, width), 0), col(8), length, True)
    scale = 1.0 / math.sqrt(length)
    c3, s3 = c3 * scale, s3 * scale
    fine_c = jnp.concatenate([c2[i : i + 1] * c3 - s2[i : i + 1] * s3 for i in range(8)], 0)
    fine_s = jnp.concatenate([s2[i : i + 1] * c3 + c2[i : i + 1] * s3 for i in range(8)], 0)
    for i in range(coarse):
        block = c1[i : i + 1] * fine_c - s1[i : i + 1] * fine_s
        table_ref[64 * i : 64 * i + 64, :] = block.astype(bf16)
    for copy in copies:
        copy.wait()
    marks = marks_of(bins_held, live_held)
    spectra = dot(held_ref[...], table_ref[...]).astype(bf16)
    nothing = jnp.zeros((slots, COLS), bf16)
    for band in range(bands):
        piece = spectra[:, band * COLS : (band + 1) * COLS]
        for tile in range(tiles):
            for t in range(SPAN):
                source = tile - 2 + t
                there = 0 <= source < tiles
                out_ref[tile, band, t * slots : (t + 1) * slots, :] = (
                    piece[source * slots : (source + 1) * slots] if there else nothing
                )
            out_ref[tile, band, SPAN * slots : SPAN * slots + 2, :] = jnp.concatenate(
                [x[tile : tile + 1] for x in marks], 0
            )


def patch_kernel(
    tiles,
    slots,
    arrived_ref,
    probe_ref,
    out_ref,
    st_ref,
    pp_ref,
    own_ref,
    gram_ref,
    sem,
):
    sources = arrived_ref.shape[0]
    per = min(BLOCK_SRC, sources)
    n = per * slots
    chunks = sources // per
    side = chunks + rim_blocks(chunks, n)
    nb = chunks + 2 * side
    pl.run_scoped(
        functools.partial(project, slots, arrived_ref, probe_ref, st_ref, pp_ref, own_ref, gram_ref),
        pltpu.VMEM((nb, COLS, n), f32),
        pltpu.VMEM((nb, 2 * RANK, n), f32),
        pltpu.VMEM((nb, ROWS, n), bf16),
        pltpu.VMEM((nb, n, ROWS), bf16),
        pltpu.VMEM((nb, n, 3 * HC), bf16),
        pltpu.VMEM((SPAN * chunks, 1, n), f32),
        pltpu.VMEM((SPAN * chunks, 8, n), f32),
    )
    invert_grams(gram_ref)
    pl.run_scoped(
        functools.partial(write, tiles, own_ref, pp_ref, gram_ref, out_ref, sem),
        pltpu.VMEM((PAIRS, COLS, 2 * HC), f32),
        pltpu.VMEM((OWN_ROWS, HC, COLS), f32),
    )


def rim_blocks(chunks, n):
    return (min(RIM * HC, chunks * n) + n - 1) // n


def over(chunks, body, carry):
    if chunks == 1:
        return body(0, carry)
    return lax.fori_loop(0, chunks, body, carry)


def project(
    slots,
    arrived_ref,
    probe_ref,
    st_ref,
    pp_ref,
    own_ref,
    gram_ref,
    vt_ref,
    wt_ref,
    ohm_ref,
    ohmt_ref,
    ohht_ref,
    rank_ref,
    fact_ref,
):
    sources = arrived_ref.shape[0]
    per = min(BLOCK_SRC, sources)
    n = per * slots
    chunks = sources // per
    members = ((0, 1), (2,), (3, 4))
    side = chunks + rim_blocks(chunks, n)
    first = (0, side, side + chunks)

    lane_src = (iota((per, n), 1) // slots == iota((per, n), 0)).astype(f32)
    before = (iota((n, n), 0) < iota((n, n), 1)).astype(f32).astype(bf16)

    def locate(chunk, totals):
        totals = list(totals)
        marks = arrived_ref[pl.ds(chunk * per, per), SPAN * slots : SPAN * slots + 2, :].astype(f32)
        facts, used = [], []
        for t in range(SPAN):
            pick = (iota((COLS, n), 0) == t * slots + iota((COLS, n), 1) % slots).astype(f32)
            pick = pick.astype(bf16)
            rows = []
            for i in range(2):
                spread = dot(marks[:, i, :].astype(bf16), pick)
                rows.append(jnp.sum(spread * lane_src, 0, keepdims=True))
            m, h = rows
            good = m < OWN_ROWS
            low, high = m < RIM, good & (m >= OWN_ROWS - RIM)
            keep = (high, good, good, good, low)[t]
            shift = (RIM - OWN_ROWS, RIM, 0, 0, OWN_ROWS)[t]
            inside = (
                (high, None, None),
                (good, high, None),
                (low, good, high),
                (None, low, good),
                (None, None, low),
            )[t]
            fact = [jnp.where(keep, m + shift + 1.0, 0.0), jnp.where(keep, h + 1.0, 0.0)]
            for ok in inside:
                fact.append(jnp.zeros_like(h) if ok is None else jnp.where(ok, h + 1.0, 0.0))
            facts.append(jnp.concatenate(fact + [jnp.zeros((3, n), f32)], 0))
            used.append(keep.astype(f32))
        use = jnp.concatenate(used + [jnp.zeros((8 - SPAN, n), f32)], 0)
        ranks = dot(use.astype(bf16), before)
        sums = jnp.sum(use, 1, keepdims=True)
        for k in range(3):
            for t in members[k]:
                rank = ranks[t : t + 1] + totals[k]
                rank_ref[t * chunks + chunk] = jnp.where(use[t : t + 1] > 0.5, rank, -1.0)
                fact_ref[t * chunks + chunk] = facts[t]
                totals[k] = totals[k] + sums[t : t + 1]
        return tuple(totals)

    zero = jnp.zeros((1, 1), f32)
    totals = over(chunks, locate, (zero, zero, zero))
    counts = [jnp.max(x).astype(jnp.int32) for x in totals]
    filled = [(c + (n - 1)) // n for c in counts]

    p_high, p_low = split(probe_ref[...])

    def pack(k, q):
        def gather(chunk, total, t):
            b = t * chunks + chunk
            wanted = iota((n, n), 0).astype(f32) + (q * n).astype(f32)
            chosen = (wanted == rank_ref[b]).astype(f32).astype(bf16)
            values = arrived_ref[pl.ds(chunk * per, per), t * slots : (t + 1) * slots, :]
            fact = jnp.concatenate([fact_ref[b], jnp.zeros((COLS - 8, n), f32)], 0).T
            both = jnp.concatenate([values.reshape(n, COLS), fact.astype(bf16)], 1)
            part = dot(chosen, both)
            return part if total is None else total + part

        total = None if chunks == 1 else jnp.zeros((n, 2 * COLS), f32)
        for t in members[k]:
            total = over(chunks, functools.partial(gather, t=t), total)
        flip = total.T
        b = first[k] + q
        vt_ref[b] = flip[:COLS]
        row, h = flip[COLS : COLS + 1] - 1.0, flip[COLS + 1 : COLS + 2] - 1.0
        column = total[:, COLS : COLS + 8] - 1.0
        ohm_ref[b] = (iota((ROWS, n), 0).astype(f32) == row).astype(f32).astype(bf16)
        ohmt_ref[b] = (iota((n, ROWS), 1).astype(f32) == column[:, 0:1]).astype(f32).astype(bf16)
        ohht_ref[b] = jnp.concatenate(
            [
                (iota((n, HC), 1).astype(f32) == column[:, 2 + p : 3 + p]).astype(f32)
                for p in range(3)
            ],
            1,
        ).astype(bf16)
        ohh = (iota((HC, n), 0).astype(f32) == h).astype(f32).astype(bf16)
        wt_ref[b] = dot(p_high, ohh) + dot(p_low, ohh)

    for k in range(3):
        pack(k, jnp.int32(0))

    for k in range(3):

        def more(q, carry, k=k):
            pack(k, q)
            return carry

        lax.fori_loop(1, filled[k], more, 0)

    st_ref[:, :, RANK:, :] = jnp.zeros((3, JG, RP - RANK, ROWS), f32)
    pp_ref[:, :, RANK:, :] = jnp.zeros((3, FDEV, RP - RANK, COLS), f32)
    lane = iota((RANK * JG, ROWS), 1)

    def step(g, carry, short):
        def sketch_of(b):
            w = wt_ref[b]
            u = []
            for j in range(JG):
                re = vt_ref[b, pl.ds(g * JG + j, 1), :]
                im = vt_ref[b, pl.ds(FDEV + g * JG + j, 1), :]
                u.append(w[:RANK] * re + w[RANK:] * im)
            return dot(jnp.concatenate(u, 0).astype(bf16), ohmt_ref[b])

        def project_of(b, rows):
            at = dot(rows, ohm_ref[b])
            z = []
            for c in range(2):
                for j in range(JG):
                    v = vt_ref[b, pl.ds(c * FDEV + g * JG + j, 1), :]
                    z.append(at[j * RANK : (j + 1) * RANK] * v)
            return dot(jnp.concatenate(z, 0).astype(bf16), ohht_ref[b])

        sketch = [sketch_of(first[k]) for k in range(3)]
        if not short:
            for k in range(3):
                sketch[k] = lax.fori_loop(
                    1, filled[k], lambda q, x, k=k: x + sketch_of(first[k] + q), sketch[k]
                )
        left, own, right = sketch
        sk = [x.astype(bf16) for x in sketch]
        proj = sum(project_of(first[k], sk[k]) for k in range(3))
        if not short:
            for k in range(3):
                proj = lax.fori_loop(
                    1, filled[k], lambda q, x, k=k: x + project_of(first[k] + q, sk[k]), proj
                )
        full_left = jnp.where(lane < ROWS - RIM, left, pltpu.roll(own, ROWS - RIM, 1))
        full_right = jnp.where(lane < ROWS - RIM, right, pltpu.roll(own, ROWS - OWN_ROWS, 1))
        full_own = jnp.where(
            lane < OWN_ROWS,
            own,
            jnp.where(lane < OWN_ROWS + RIM, left, pltpu.roll(right, ROWS - RIM, 1)),
        )
        half = RANK * JG
        re, im = proj[:half], proj[half:]
        lo = iota((half, COLS), 1) < HC
        parts = [
            jnp.where(lo, re[:, :COLS], pltpu.roll(im[:, :COLS], HC, 1)),
            jnp.where(lo, pltpu.roll(re[:, :COLS], HC, 1), im[:, :COLS]),
            jnp.where(
                lo,
                jnp.concatenate([re[:, COLS:], re[:, COLS:]], 1),
                jnp.concatenate([im[:, COLS:], im[:, COLS:]], 1),
            ),
        ]
        for p, whole in enumerate((full_left, full_own, full_right)):
            st_ref[p, :, :RANK, :] = whole.reshape(JG, RANK, ROWS)
            pp_ref[p, pl.ds(g * JG, JG), :RANK, :] = parts[p].reshape(JG, RANK, COLS)
            pad = st_ref[p].reshape(JG * RP, ROWS).astype(bf16)
            if p == 1:
                for q2 in range(2):
                    quad = st_ref[p, 4 * q2 : 4 * q2 + 4].reshape(4 * RP, ROWS)
                    own_ref[2 * g + q2] = quad.T
            gram = lax.dot_general(pad, pad, (((1,), (1,)), ((), ())), preferred_element_type=f32)
            for q2 in range(2):
                lanes = iota((RANK, 4 * RP), 1) // RP
                acc = jnp.zeros((RANK, 4 * RP), f32)
                for q in range(4):
                    at = (q2 * 4 + q) * RP
                    piece = gram[at : at + RANK, q2 * 4 * RP : (q2 + 1) * 4 * RP]
                    acc = jnp.where(lanes == q, piece, acc)
                gram_ref[p * (FDEV // 4) + 2 * g + q2] = acc
        return carry

    one_block = jnp.maximum(jnp.maximum(filled[0], filled[1]), filled[2]) <= 1

    @pl.when(one_block)
    def _():
        lax.fori_loop(0, FDEV // JG, functools.partial(step, short=True), 0, unroll=4)

    @pl.when(jnp.logical_not(one_block))
    def _():
        lax.fori_loop(0, FDEV // JG, functools.partial(step, short=False), 0)


def invert_grams(gram_ref):
    count = 3 * FDEV // 4
    batch = 48
    wide = 4 * RP
    lane3 = iota((batch, RANK, wide), 2) % RP
    row3 = iota((batch, RANK, wide), 1)
    lane1 = iota((batch, 1, wide), 2) % RP
    base = iota((batch * RANK, wide), 1) // RP * RP
    same = (iota((wide, wide), 0) // RP == iota((wide, wide), 1) // RP).astype(f32)

    def invert(i, carry):
        a = gram_ref[pl.ds(i * batch, batch)]
        diag = jnp.sum(jnp.where(lane3 == row3, a, 0.0), 1)
        trace = jnp.dot(
            diag, same, preferred_element_type=f32, precision=lax.Precision.HIGHEST
        )
        ridge = 0.01 * trace / RANK + 1e-06
        a = a + jnp.where(lane3 == row3, ridge[:, None, :], 0.0)
        for k in range(0, RANK, 2):
            flat = a.reshape(batch * RANK, wide)
            c0 = jnp.take_along_axis(flat, base + k, axis=1).reshape(batch, RANK, wide)
            c1 = jnp.take_along_axis(flat, base + k + 1, axis=1).reshape(batch, RANK, wide)
            x, y, z = c0[:, k : k + 1], c1[:, k : k + 1], c1[:, k + 1 : k + 2]
            scale = 1.0 / (x * z - y * y)
            x, y, z = z * scale, -y * scale, x * scale
            r0, r1 = a[:, k : k + 1], a[:, k + 1 : k + 2]
            n0 = jnp.where(lane1 == k, x, jnp.where(lane1 == k + 1, y, x * r0 + y * r1))
            n1 = jnp.where(lane1 == k, y, jnp.where(lane1 == k + 1, z, y * r0 + z * r1))
            a = jnp.where(lane3 // 2 == k // 2, 0.0, a) - c0 * n0 - c1 * n1
            a = jnp.where(row3 == k, n0, jnp.where(row3 == k + 1, n1, a))
        gram_ref[pl.ds(i * batch, batch)] = a
        return carry

    lax.fori_loop(0, count // batch, invert, 0)


def write(tiles, own_ref, pp_ref, gram_ref, out_ref, sem, freq_ref, cells_ref):
    count = FDEV // 4
    wide = 4 * RP
    here = lax.axis_index("grid")
    has_left = (here > 0).astype(f32)
    has_right = (here < tiles - 1).astype(f32)
    rim = RIM // 2
    edge = iota((rim * JG, 1), 0) < MY // 2 * JG
    taper_first = jnp.where(edge, 0.6, 0.8)
    taper_last = jnp.where(edge, 0.8, 0.6)
    left_w = jnp.where(edge, 0.4, 0.2) * has_left
    right_w = jnp.where(edge, 0.2, 0.4) * has_right
    lo = iota((wide, COLS), 1) < HC
    mine = [iota((JG, wide), 1) // RP + 4 * q2 == iota((JG, wide), 0) for q2 in range(2)]

    def rebuild(g, carry):
        rows = []
        for m in range(PAIRS):
            row = []
            for parity in range(2):
                for q2 in range(2):
                    x = own_ref[2 * g + q2, pl.ds(2 * m + parity, 1), :]
                    row.append(jnp.where(mine[q2], x, 0.0))
            rows.append(jnp.concatenate(row, 1))
        rows = jnp.concatenate(rows, 0).astype(bf16)
        w = []
        for p in range(3):
            even, odd = [], []
            for q2 in range(2):
                i = 2 * g + q2
                inverse = gram_ref[p * count + i]
                lanes = iota((RANK, wide), 1) // RP
                zero = jnp.zeros((RP - RANK, wide), f32)
                diag = []
                for q in range(4):
                    diag += [jnp.where(lanes == q, inverse, 0.0), zero]
                b_high, b_low = split(jnp.concatenate(diag, 0))
                p_high, p_low = split(pp_ref[p, pl.ds(i * 4, 4)].reshape(wide, COLS))
                twice = dot(b_high, jnp.concatenate([p_high, p_low], 1))
                c = twice[:, :COLS] + twice[:, COLS:] + dot(b_low, p_high)
                r = pltpu.roll(c, HC, 1)
                even.append(jnp.concatenate([jnp.where(lo, c, 0.0), jnp.where(lo, r, 0.0)], 1))
                odd.append(jnp.concatenate([jnp.where(lo, 0.0, r), jnp.where(lo, 0.0, c)], 1))
            w.append(jnp.concatenate(even + odd, 0).astype(bf16))
        mid = dot(rows, w[1])
        first, last = rim * JG, (PAIRS - rim) * JG
        begin = mid[:first] * taper_first + dot(rows[:first], w[0]) * left_w
        end = mid[last:] * taper_last + dot(rows[last:], w[2]) * right_w
        full = jnp.concatenate([begin, mid[first:last], end], 0)
        for c in range(2):
            part = full[:, c * COLS : (c + 1) * COLS].reshape(PAIRS, JG, COLS)
            freq_ref[:, pl.ds(pl.multiple_of(c * FDEV + g * JG, JG), JG), :] = part
        return carry

    lax.fori_loop(0, FDEV // JG, rebuild, 0, unroll=2)

    unroll = 8

    def turn(i, carry):
        for q in range(unroll):
            m = i * unroll + q
            flip = freq_ref[m].T
            cells_ref[pl.ds(2 * m, 2)] = flip.reshape(2, HC, COLS)
        return carry

    pieces = 6
    size = OWN_ROWS // pieces
    copies = []
    for k in range(pieces):
        per_piece = size // (2 * unroll)
        lax.fori_loop(k * per_piece, (k + 1) * per_piece, turn, 0)
        copy = pltpu.make_async_copy(
            cells_ref.at[pl.ds(k * size, size)], out_ref.at[pl.ds(k * size, size)], sem.at[k]
        )
        copy.start()
        copies.append(copy)
    for copy in copies:
        copy.wait()


def patches(arrived, probe, tiles, slots):
    return pl.pallas_call(
        functools.partial(patch_kernel, tiles, slots),
        out_shape=jax.ShapeDtypeStruct((OWN_ROWS, HC, COLS), f32),
        in_specs=[pl.BlockSpec(memory_space=pltpu.VMEM)] * 2,
        out_specs=pl.BlockSpec(memory_space=pl.ANY),
        scratch_shapes=[
            pltpu.VMEM((3, JG, RP, ROWS), f32),
            pltpu.VMEM((3, FDEV, RP, COLS), f32),
            pltpu.VMEM((FDEV // 4, ROWS, 4 * RP), f32),
            pltpu.VMEM((3 * FDEV // 4, RANK, 4 * RP), f32),
            pltpu.SemaphoreType.DMA((6,)),
        ],
        compiler_params=pltpu.CompilerParams(vmem_limit_bytes=60 * 2**20),
        name="patches",
    )(arrived, probe)


def per_device(traces, bins, live, probe):
    tiles = lax.axis_size("grid")
    bands = lax.axis_size("freq")
    slots, length = traces.shape[2:]
    sources = tiles * bands
    used = SPAN * slots

    vmem = pl.BlockSpec(memory_space=pltpu.VMEM)
    sent = pl.pallas_call(
        spectra_kernel,
        out_shape=jax.ShapeDtypeStruct((tiles, bands, used + 2, COLS), bf16),
        in_specs=[pl.BlockSpec(memory_space=pl.ANY)] * 3,
        out_specs=vmem,
        scratch_shapes=[
            pltpu.VMEM((length, COLS * bands), bf16),
            pltpu.VMEM((tiles * slots, length), bf16),
            pltpu.VMEM((tiles, slots), jnp.int32),
            pltpu.VMEM((tiles, slots), jnp.int32),
            pltpu.SemaphoreType.DMA((3,)),
        ],
        compiler_params=pltpu.CompilerParams(vmem_limit_bytes=60 * 2**20),
        name="spectra",
    )(traces.reshape(tiles * slots, length), bins[0], live[0])

    arrived = lax.all_to_all(
        sent.reshape(sources, used + 2, COLS), ("grid", "freq"), 0, 0, tiled=True
    )

    out = patches(
        arrived, jnp.transpose(probe, (1, 2, 0)).reshape(2 * RANK, HC), tiles, slots
    )
    return out.reshape(OWNX, MY, HC, COLS)


def solution(mesh):
    placed = (
        P(("grid", "freq"), None, None, None),
        P(("grid", "freq"), None, None),
        P(("grid", "freq"), None, None),
        P(),
    )
    return jax.shard_map(
        per_device,
        mesh=mesh,
        in_specs=placed,
        out_specs=P("grid", None, None, "freq"),
        check_vma=False,
    )
```

```python
import functools
import math

import jax
import jax.numpy as jnp
from jax import lax
from jax.experimental import pallas as pl
from jax.experimental.pallas import tpu as pltpu
from jax.sharding import PartitionSpec as P

FDEV = 64
FIRST = 8
PX = 16
MY = 16
HC = 64
MARGIN = 2
OWNX = 12
RANK = 24
SPAN = 5
OWN_ROWS = OWNX * MY
RIM = MARGIN * MY
ROWS = PX * MY
PAIRS = OWN_ROWS // 2
COLS = 2 * FDEV
JG = 8
RP = 32
BLOCK_SRC = 32
DEAD = 255.0
UNROLL = 4
PER_STEP = 3

f32 = jnp.float32
bf16 = jnp.bfloat16


def dot(a, b):
    return jnp.dot(a, b, preferred_element_type=f32)


def split(x):
    high = x.astype(bf16)
    return high, (x - high.astype(f32)).astype(bf16)


def iota(shape, dim):
    return lax.broadcasted_iota(jnp.int32, shape, dim)


def phase(times, columns, length, quarter):
    k = FIRST + columns // COLS * FDEV + columns % FDEV
    turns = ((times * k) & (length - 1)).astype(f32)
    angle = turns * (2.0 * math.pi / length)
    if quarter:
        angle = angle + (columns // FDEV % 2).astype(f32) * (0.5 * math.pi)
    return jnp.cos(angle), jnp.sin(angle)


def marks_of(bins_ref, live_ref):
    tiles, slots = bins_ref.shape
    on = live_ref[...] == 1
    both = jnp.concatenate(
        [
            jnp.where(on, bins_ref[...] // HC, int(DEAD)),
            jnp.where(on, bins_ref[...] % HC, 0),
        ],
        0,
    )
    lanes = iota((slots, SPAN * COLS), 1)
    put = (lanes % COLS == lanes // COLS * slots + iota((slots, SPAN * COLS), 0)).astype(f32)
    placed = dot(both.astype(f32).astype(bf16), put.astype(bf16))
    tile, lane = iota((tiles, COLS), 0), iota((tiles, COLS), 1)
    marks = []
    for i, other in enumerate((DEAD, 0.0)):
        mark = jnp.full((tiles, COLS), other, f32)
        for t in range(SPAN):
            moved = placed[i * tiles : (i + 1) * tiles, t * COLS : (t + 1) * COLS]
            if t != 2:
                moved = pltpu.roll(moved, (2 - t) % tiles, 0)
            there = (tile + (t - 2) >= 0) & (tile + (t - 2) < tiles) & (lane // slots == t)
            mark = jnp.where(there, moved, mark)
        marks.append(mark.astype(bf16))
    return marks


def spectra_kernel(
    traces_ref, bins_ref, live_ref, out_ref, table_ref, held_ref, bins_held, live_held, sem
):
    length, width = table_ref.shape
    tiles, bands = out_ref.shape[:2]
    slots = bins_ref.shape[1]
    moves = ((bins_ref, bins_held), (live_ref, live_held), (traces_ref, held_ref))
    copies = [pltpu.make_async_copy(a, b, sem.at[i]) for i, (a, b) in enumerate(moves)]
    for copy in copies:
        copy.start()
    coarse = length // 64
    column = iota((1, width), 1)
    col = lambda n: column + jnp.zeros((n, 1), jnp.int32)
    c1, s1 = phase(iota((coarse, width), 0) * 64, col(coarse), length, False)
    c2, s2 = phase(iota((8, width), 0) * 8, col(8), length, False)
    c3, s3 = phase(iota((8, width), 0), col(8), length, True)
    scale = 1.0 / math.sqrt(length)
    c3, s3 = c3 * scale, s3 * scale
    fine_c = jnp.concatenate([c2[i : i + 1] * c3 - s2[i : i + 1] * s3 for i in range(8)], 0)
    fine_s = jnp.concatenate([s2[i : i + 1] * c3 + c2[i : i + 1] * s3 for i in range(8)], 0)
    for i in range(coarse):
        block = c1[i : i + 1] * fine_c - s1[i : i + 1] * fine_s
        table_ref[64 * i : 64 * i + 64, :] = block.astype(bf16)
    for copy in copies:
        copy.wait()
    marks = marks_of(bins_held, live_held)
    spectra = dot(held_ref[...], table_ref[...]).astype(bf16)
    nothing = jnp.zeros((slots, COLS), bf16)
    for band in range(bands):
        piece = spectra[:, band * COLS : (band + 1) * COLS]
        for tile in range(tiles):
            for t in range(SPAN):
                source = tile - 2 + t
                there = 0 <= source < tiles
                out_ref[tile, band, t * slots : (t + 1) * slots, :] = (
                    piece[source * slots : (source + 1) * slots] if there else nothing
                )
            out_ref[tile, band, SPAN * slots : SPAN * slots + 2, :] = jnp.concatenate(
                [x[tile : tile + 1] for x in marks], 0
            )


def patch_kernel(
    tiles,
    slots,
    arrived_ref,
    probe_ref,
    out_ref,
    st_ref,
    pp_ref,
    own_ref,
    first_ref,
    second_ref,
    sem,
):
    sources = arrived_ref.shape[0]
    per = min(BLOCK_SRC, sources)
    n = per * slots
    chunks = sources // per
    side = chunks + rim_blocks(chunks, n)
    nb = chunks + 2 * side
    pl.run_scoped(
        functools.partial(
            project, slots, arrived_ref, probe_ref, st_ref, pp_ref, own_ref, first_ref, second_ref
        ),
        pltpu.VMEM((nb, COLS, n), f32),
        pltpu.VMEM((nb, 2 * RANK, n), f32),
        pltpu.VMEM((nb, ROWS, n), bf16),
        pltpu.VMEM((nb, n, ROWS), bf16),
        pltpu.VMEM((nb, n, 3 * HC), bf16),
        pltpu.VMEM((SPAN * chunks, 1, n), f32),
        pltpu.VMEM((SPAN * chunks, 8, n), f32),
    )
    pl.run_scoped(
        functools.partial(write, tiles, own_ref, pp_ref, first_ref, second_ref, out_ref, sem),
        pltpu.VMEM((PAIRS, COLS, 2 * HC), f32),
        pltpu.VMEM((OWN_ROWS, HC, COLS), f32),
    )


def rim_blocks(chunks, n):
    return (min(RIM * HC, chunks * n) + n - 1) // n


def over(chunks, body, carry):
    if chunks == 1:
        return body(0, carry)
    return lax.fori_loop(0, chunks, body, carry)


def project(
    slots,
    arrived_ref,
    probe_ref,
    st_ref,
    pp_ref,
    own_ref,
    first_ref,
    second_ref,
    vt_ref,
    wt_ref,
    ohm_ref,
    ohmt_ref,
    ohht_ref,
    rank_ref,
    fact_ref,
):
    sources = arrived_ref.shape[0]
    per = min(BLOCK_SRC, sources)
    n = per * slots
    chunks = sources // per
    members = ((0, 1), (2,), (3, 4))
    side = chunks + rim_blocks(chunks, n)
    first = (0, side, side + chunks)

    lane_src = (iota((per, n), 1) // slots == iota((per, n), 0)).astype(f32)
    before = (iota((n, n), 0) < iota((n, n), 1)).astype(f32).astype(bf16)

    def locate(chunk, totals):
        totals = list(totals)
        marks = arrived_ref[pl.ds(chunk * per, per), SPAN * slots : SPAN * slots + 2, :].astype(f32)
        facts, used = [], []
        for t in range(SPAN):
            pick = (iota((COLS, n), 0) == t * slots + iota((COLS, n), 1) % slots).astype(f32)
            pick = pick.astype(bf16)
            rows = []
            for i in range(2):
                spread = dot(marks[:, i, :].astype(bf16), pick)
                rows.append(jnp.sum(spread * lane_src, 0, keepdims=True))
            m, h = rows
            good = m < OWN_ROWS
            low, high = m < RIM, good & (m >= OWN_ROWS - RIM)
            keep = (high, good, good, good, low)[t]
            shift = (RIM - OWN_ROWS, RIM, 0, 0, OWN_ROWS)[t]
            inside = (
                (high, None, None),
                (good, high, None),
                (low, good, high),
                (None, low, good),
                (None, None, low),
            )[t]
            fact = [jnp.where(keep, m + shift + 1.0, 0.0), jnp.where(keep, h + 1.0, 0.0)]
            for ok in inside:
                fact.append(jnp.zeros_like(h) if ok is None else jnp.where(ok, h + 1.0, 0.0))
            facts.append(jnp.concatenate(fact + [jnp.zeros((3, n), f32)], 0))
            used.append(keep.astype(f32))
        use = jnp.concatenate(used + [jnp.zeros((8 - SPAN, n), f32)], 0)
        ranks = dot(use.astype(bf16), before)
        sums = jnp.sum(use, 1, keepdims=True)
        for k in range(3):
            for t in members[k]:
                rank = ranks[t : t + 1] + totals[k]
                rank_ref[t * chunks + chunk] = jnp.where(use[t : t + 1] > 0.5, rank, -1.0)
                fact_ref[t * chunks + chunk] = facts[t]
                totals[k] = totals[k] + sums[t : t + 1]
        return tuple(totals)

    zero = jnp.zeros((1, 1), f32)
    totals = over(chunks, locate, (zero, zero, zero))
    counts = [jnp.max(x).astype(jnp.int32) for x in totals]
    filled = [(c + (n - 1)) // n for c in counts]

    p_high, p_low = split(probe_ref[...])

    def pack(k, q):
        def gather(chunk, total, t):
            b = t * chunks + chunk
            wanted = iota((n, n), 0).astype(f32) + (q * n).astype(f32)
            chosen = (wanted == rank_ref[b]).astype(f32).astype(bf16)
            values = arrived_ref[pl.ds(chunk * per, per), t * slots : (t + 1) * slots, :]
            fact = jnp.concatenate([fact_ref[b], jnp.zeros((COLS - 8, n), f32)], 0).T
            both = jnp.concatenate([values.reshape(n, COLS), fact.astype(bf16)], 1)
            part = dot(chosen, both)
            return part if total is None else total + part

        total = None if chunks == 1 else jnp.zeros((n, 2 * COLS), f32)
        for t in members[k]:
            total = over(chunks, functools.partial(gather, t=t), total)
        flip = total.T
        b = first[k] + q
        vt_ref[b] = flip[:COLS]
        row, h = flip[COLS : COLS + 1] - 1.0, flip[COLS + 1 : COLS + 2] - 1.0
        column = total[:, COLS : COLS + 8] - 1.0
        ohm_ref[b] = (iota((ROWS, n), 0).astype(f32) == row).astype(f32).astype(bf16)
        ohmt_ref[b] = (iota((n, ROWS), 1).astype(f32) == column[:, 0:1]).astype(f32).astype(bf16)
        ohht_ref[b] = jnp.concatenate(
            [
                (iota((n, HC), 1).astype(f32) == column[:, 2 + p : 3 + p]).astype(f32)
                for p in range(3)
            ],
            1,
        ).astype(bf16)
        ohh = (iota((HC, n), 0).astype(f32) == h).astype(f32).astype(bf16)
        wt_ref[b] = dot(p_high, ohh) + dot(p_low, ohh)

    for k in range(3):
        pack(k, jnp.int32(0))

    for k in range(3):

        def more(q, carry, k=k):
            pack(k, q)
            return carry

        lax.fori_loop(1, filled[k], more, 0)

    st_ref[:, :, RANK:, :] = jnp.zeros((3, JG, RP - RANK, ROWS), f32)
    pp_ref[:, :, RANK:, :] = jnp.zeros((3, FDEV, RP - RANK, COLS), f32)
    lane = iota((RANK * JG, ROWS), 1)

    def step(g, carry, short, gram_ref, start):
        def sketch_of(b):
            w = wt_ref[b]
            u = []
            for j in range(JG):
                re = vt_ref[b, pl.ds(g * JG + j, 1), :]
                im = vt_ref[b, pl.ds(FDEV + g * JG + j, 1), :]
                u.append(w[:RANK] * re + w[RANK:] * im)
            return dot(jnp.concatenate(u, 0).astype(bf16), ohmt_ref[b])

        def project_of(b, rows):
            at = dot(rows, ohm_ref[b])
            z = []
            for c in range(2):
                for j in range(JG):
                    v = vt_ref[b, pl.ds(c * FDEV + g * JG + j, 1), :]
                    z.append(at[j * RANK : (j + 1) * RANK] * v)
            return dot(jnp.concatenate(z, 0).astype(bf16), ohht_ref[b])

        sketch = [sketch_of(first[k]) for k in range(3)]
        if not short:
            for k in range(3):
                sketch[k] = lax.fori_loop(
                    1, filled[k], lambda q, x, k=k: x + sketch_of(first[k] + q), sketch[k]
                )
        left, own, right = sketch
        sk = [x.astype(bf16) for x in sketch]
        proj = sum(project_of(first[k], sk[k]) for k in range(3))
        if not short:
            for k in range(3):
                proj = lax.fori_loop(
                    1, filled[k], lambda q, x, k=k: x + project_of(first[k] + q, sk[k]), proj
                )
        full_left = jnp.where(lane < ROWS - RIM, left, pltpu.roll(own, ROWS - RIM, 1))
        full_right = jnp.where(lane < ROWS - RIM, right, pltpu.roll(own, ROWS - OWN_ROWS, 1))
        full_own = jnp.where(
            lane < OWN_ROWS,
            own,
            jnp.where(lane < OWN_ROWS + RIM, left, pltpu.roll(right, ROWS - RIM, 1)),
        )
        half = RANK * JG
        re, im = proj[:half], proj[half:]
        lo = iota((half, COLS), 1) < HC
        parts = [
            jnp.where(lo, re[:, :COLS], pltpu.roll(im[:, :COLS], HC, 1)),
            jnp.where(lo, pltpu.roll(re[:, :COLS], HC, 1), im[:, :COLS]),
            jnp.where(
                lo,
                jnp.concatenate([re[:, COLS:], re[:, COLS:]], 1),
                jnp.concatenate([im[:, COLS:], im[:, COLS:]], 1),
            ),
        ]
        for p, whole in enumerate((full_left, full_own, full_right)):
            st_ref[p, :, :RANK, :] = whole.reshape(JG, RANK, ROWS)
            pp_ref[p, pl.ds(g * JG, JG), :RANK, :] = parts[p].reshape(JG, RANK, COLS)
            pad = st_ref[p].reshape(JG * RP, ROWS).astype(bf16)
            if p == 1:
                for q2 in range(2):
                    quad = st_ref[p, 4 * q2 : 4 * q2 + 4].reshape(4 * RP, ROWS)
                    own_ref[2 * g + q2] = quad.T
            gram = lax.dot_general(pad, pad, (((1,), (1,)), ((), ())), preferred_element_type=f32)
            for q2 in range(2):
                lanes = iota((RANK, 4 * RP), 1) // RP
                acc = jnp.zeros((RANK, 4 * RP), f32)
                for q in range(4):
                    at = (q2 * 4 + q) * RP
                    piece = gram[at : at + RANK, q2 * 4 * RP : (q2 + 1) * 4 * RP]
                    acc = jnp.where(lanes == q, piece, acc)
                gram_ref[:, p * (FDEV // 8) + 2 * (g - start) + q2, :] = acc
        return carry

    one_block = jnp.maximum(jnp.maximum(filled[0], filled[1]), filled[2]) <= 1

    steps = FDEV // JG
    half = steps // 2

    @pl.when(one_block)
    def _():
        early = functools.partial(step, short=True, gram_ref=first_ref, start=0)
        lax.fori_loop(0, half, early, 0, unroll=UNROLL)
        work = invert(first_ref)
        for g in range(half, steps):
            for _ in range(PER_STEP):
                next(work, None)
            step(g, 0, True, second_ref, half)
        for _ in work:
            pass

    @pl.when(jnp.logical_not(one_block))
    def _():
        for i, ref in enumerate((first_ref, second_ref)):
            body = functools.partial(step, short=False, gram_ref=ref, start=i * half)
            lax.fori_loop(i * half, (i + 1) * half, body, 0)
        for _ in invert(first_ref):
            pass


def invert(gram_ref):
    wide = 4 * RP
    count = gram_ref.shape[1]
    lane = iota((count, wide), 1) % RP
    base = iota((count, wide), 1) // RP * RP
    same = (iota((wide, wide), 0) // RP == iota((wide, wide), 1) // RP).astype(f32)
    a = [gram_ref[r] for r in range(RANK)]
    diag = jnp.zeros((count, wide), f32)
    for r in range(RANK):
        diag = jnp.where(lane == r, a[r], diag)
    trace = jnp.dot(diag, same, preferred_element_type=f32, precision=lax.Precision.HIGHEST)
    ridge = 0.01 * trace / RANK + 1e-06
    a = [jnp.where(lane == r, a[r] + ridge, a[r]) for r in range(RANK)]
    for k in range(0, RANK, 2):
        c0 = [jnp.take_along_axis(x, base + k, axis=1) for x in a]
        c1 = [jnp.take_along_axis(x, base + (k + 1), axis=1) for x in a]
        x, y, z = c0[k], c1[k], c1[k + 1]
        scale = 1.0 / (x * z - y * y)
        x, y, z = z * scale, -y * scale, x * scale
        n0 = jnp.where(lane == k, x, jnp.where(lane == k + 1, y, x * a[k] + y * a[k + 1]))
        n1 = jnp.where(lane == k, y, jnp.where(lane == k + 1, z, y * a[k] + z * a[k + 1]))
        pair = lane // 2 == k // 2
        for r in range(RANK):
            if r // 2 != k // 2:
                a[r] = jnp.where(pair, 0.0, a[r]) - c0[r] * n0 - c1[r] * n1
        a[k], a[k + 1] = n0, n1
        yield
    for r in range(RANK):
        gram_ref[r] = a[r]


def write(
    tiles, own_ref, pp_ref, first_ref, second_ref, out_ref, sem, freq_ref, cells_ref
):
    count = FDEV // 4
    wide = 4 * RP
    here = lax.axis_index("grid")
    has_left = (here > 0).astype(f32)
    has_right = (here < tiles - 1).astype(f32)
    rim = RIM // 2
    edge = iota((rim * JG, 1), 0) < MY // 2 * JG
    taper_first = jnp.where(edge, 0.6, 0.8)
    taper_last = jnp.where(edge, 0.8, 0.6)
    left_w = jnp.where(edge, 0.4, 0.2) * has_left
    right_w = jnp.where(edge, 0.2, 0.4) * has_right
    lo = iota((wide, COLS), 1) < HC
    mine = [iota((JG, wide), 1) // RP + 4 * q2 == iota((JG, wide), 0) for q2 in range(2)]

    def rebuild(g, carry, gram_ref, start):
        rows = []
        for m in range(PAIRS):
            row = []
            for parity in range(2):
                for q2 in range(2):
                    x = own_ref[2 * g + q2, pl.ds(2 * m + parity, 1), :]
                    row.append(jnp.where(mine[q2], x, 0.0))
            rows.append(jnp.concatenate(row, 1))
        rows = jnp.concatenate(rows, 0).astype(bf16)
        w = []
        for p in range(3):
            even, odd = [], []
            for q2 in range(2):
                i = 2 * g + q2
                inverse = gram_ref[:, p * (FDEV // 8) + i - 2 * start, :]
                lanes = iota((RANK, wide), 1) // RP
                zero = jnp.zeros((RP - RANK, wide), f32)
                diag = []
                for q in range(4):
                    diag += [jnp.where(lanes == q, inverse, 0.0), zero]
                b_high, b_low = split(jnp.concatenate(diag, 0))
                p_high, p_low = split(pp_ref[p, pl.ds(i * 4, 4)].reshape(wide, COLS))
                twice = dot(b_high, jnp.concatenate([p_high, p_low], 1))
                c = twice[:, :COLS] + twice[:, COLS:] + dot(b_low, p_high)
                r = pltpu.roll(c, HC, 1)
                even.append(jnp.concatenate([jnp.where(lo, c, 0.0), jnp.where(lo, r, 0.0)], 1))
                odd.append(jnp.concatenate([jnp.where(lo, 0.0, r), jnp.where(lo, 0.0, c)], 1))
            w.append(jnp.concatenate(even + odd, 0).astype(bf16))
        mid = dot(rows, w[1])
        first, last = rim * JG, (PAIRS - rim) * JG
        begin = mid[:first] * taper_first + dot(rows[:first], w[0]) * left_w
        end = mid[last:] * taper_last + dot(rows[last:], w[2]) * right_w
        full = jnp.concatenate([begin, mid[first:last], end], 0)
        for c in range(2):
            part = full[:, c * COLS : (c + 1) * COLS].reshape(PAIRS, JG, COLS)
            freq_ref[:, pl.ds(pl.multiple_of(c * FDEV + g * JG, JG), JG), :] = part
        return carry

    steps = FDEV // JG
    half = steps // 2
    work = invert(second_ref)
    for g in range(half):
        for _ in range(PER_STEP):
            next(work, None)
        rebuild(g, 0, first_ref, 0)
    for _ in work:
        pass
    late = functools.partial(rebuild, gram_ref=second_ref, start=half)
    lax.fori_loop(half, steps, late, 0, unroll=2)

    unroll = 8

    def turn(i, carry):
        for q in range(unroll):
            m = i * unroll + q
            flip = freq_ref[m].T
            cells_ref[pl.ds(2 * m, 2)] = flip.reshape(2, HC, COLS)
        return carry

    pieces = 6
    size = OWN_ROWS // pieces
    copies = []
    for k in range(pieces):
        per_piece = size // (2 * unroll)
        lax.fori_loop(k * per_piece, (k + 1) * per_piece, turn, 0)
        copy = pltpu.make_async_copy(
            cells_ref.at[pl.ds(k * size, size)], out_ref.at[pl.ds(k * size, size)], sem.at[k]
        )
        copy.start()
        copies.append(copy)
    for copy in copies:
        copy.wait()


def patches(arrived, probe, tiles, slots):
    return pl.pallas_call(
        functools.partial(patch_kernel, tiles, slots),
        out_shape=jax.ShapeDtypeStruct((OWN_ROWS, HC, COLS), f32),
        in_specs=[pl.BlockSpec(memory_space=pltpu.VMEM)] * 2,
        out_specs=pl.BlockSpec(memory_space=pl.ANY),
        scratch_shapes=[
            pltpu.VMEM((3, JG, RP, ROWS), f32),
            pltpu.VMEM((3, FDEV, RP, COLS), f32),
            pltpu.VMEM((FDEV // 4, ROWS, 4 * RP), f32),
            pltpu.VMEM((RANK, 3 * FDEV // 8, 4 * RP), f32),
            pltpu.VMEM((RANK, 3 * FDEV // 8, 4 * RP), f32),
            pltpu.SemaphoreType.DMA((6,)),
        ],
        compiler_params=pltpu.CompilerParams(vmem_limit_bytes=60 * 2**20),
        name="patches",
    )(arrived, probe)


def per_device(traces, bins, live, probe):
    tiles = lax.axis_size("grid")
    bands = lax.axis_size("freq")
    slots, length = traces.shape[2:]
    sources = tiles * bands
    used = SPAN * slots

    vmem = pl.BlockSpec(memory_space=pltpu.VMEM)
    sent = pl.pallas_call(
        spectra_kernel,
        out_shape=jax.ShapeDtypeStruct((tiles, bands, used + 2, COLS), bf16),
        in_specs=[pl.BlockSpec(memory_space=pl.ANY)] * 3,
        out_specs=vmem,
        scratch_shapes=[
            pltpu.VMEM((length, COLS * bands), bf16),
            pltpu.VMEM((tiles * slots, length), bf16),
            pltpu.VMEM((tiles, slots), jnp.int32),
            pltpu.VMEM((tiles, slots), jnp.int32),
            pltpu.SemaphoreType.DMA((3,)),
        ],
        compiler_params=pltpu.CompilerParams(vmem_limit_bytes=60 * 2**20),
        name="spectra",
    )(traces.reshape(tiles * slots, length), bins[0], live[0])

    arrived = lax.all_to_all(
        sent.reshape(sources, used + 2, COLS), ("grid", "freq"), 0, 0, tiled=True
    )

    out = patches(
        arrived, jnp.transpose(probe, (1, 2, 0)).reshape(2 * RANK, HC), tiles, slots
    )
    return out.reshape(OWNX, MY, HC, COLS)


def solution(mesh):
    placed = (
        P(("grid", "freq"), None, None, None),
        P(("grid", "freq"), None, None),
        P(("grid", "freq"), None, None),
        P(),
    )
    return jax.shard_map(
        per_device,
        mesh=mesh,
        in_specs=placed,
        out_specs=P("grid", None, None, "freq"),
        check_vma=False,
    )
```

```python
import functools
import math

import jax
import jax.numpy as jnp
from jax import lax
from jax.experimental import pallas as pl
from jax.experimental.pallas import tpu as pltpu
from jax.sharding import PartitionSpec as P

FDEV = 64
FIRST = 8
PX = 16
MY = 16
HC = 64
MARGIN = 2
OWNX = 12
RANK = 24
SPAN = 5
OWN_ROWS = OWNX * MY
RIM = MARGIN * MY
ROWS = PX * MY
PAIRS = OWN_ROWS // 2
COLS = 2 * FDEV
JG = 8
RP = 32
BLOCK_SRC = 32
DEAD = 255.0
UNROLL = 4
PER_STEP = 3

f32 = jnp.float32
bf16 = jnp.bfloat16


def dot(a, b):
    return jnp.dot(a, b, preferred_element_type=f32)


def split(x):
    high = x.astype(bf16)
    return high, (x - high.astype(f32)).astype(bf16)


def iota(shape, dim):
    return lax.broadcasted_iota(jnp.int32, shape, dim)


def phase(times, columns, length, quarter):
    k = FIRST + columns // COLS * FDEV + columns % FDEV
    turns = ((times * k) & (length - 1)).astype(f32)
    angle = turns * (2.0 * math.pi / length)
    if quarter:
        angle = angle + (columns // FDEV % 2).astype(f32) * (0.5 * math.pi)
    return jnp.cos(angle), jnp.sin(angle)


def marks_of(bins_ref, live_ref):
    tiles, slots = bins_ref.shape
    on = live_ref[...] == 1
    both = jnp.concatenate(
        [
            jnp.where(on, bins_ref[...] // HC, int(DEAD)),
            jnp.where(on, bins_ref[...] % HC, 0),
        ],
        0,
    )
    lanes = iota((slots, SPAN * COLS), 1)
    put = (lanes % COLS == lanes // COLS * slots + iota((slots, SPAN * COLS), 0)).astype(f32)
    placed = dot(both.astype(f32).astype(bf16), put.astype(bf16))
    tile, lane = iota((tiles, COLS), 0), iota((tiles, COLS), 1)
    marks = []
    for i, other in enumerate((DEAD, 0.0)):
        mark = jnp.full((tiles, COLS), other, f32)
        for t in range(SPAN):
            moved = placed[i * tiles : (i + 1) * tiles, t * COLS : (t + 1) * COLS]
            if t != 2:
                moved = pltpu.roll(moved, (2 - t) % tiles, 0)
            there = (tile + (t - 2) >= 0) & (tile + (t - 2) < tiles) & (lane // slots == t)
            mark = jnp.where(there, moved, mark)
        marks.append(mark.astype(bf16))
    return marks


def spectra_kernel(
    traces_ref, bins_ref, live_ref, out_ref, table_ref, held_ref, bins_held, live_held, sem
):
    length, width = table_ref.shape
    tiles, bands = out_ref.shape[:2]
    slots = bins_ref.shape[1]
    moves = ((bins_ref, bins_held), (live_ref, live_held), (traces_ref, held_ref))
    copies = [pltpu.make_async_copy(a, b, sem.at[i]) for i, (a, b) in enumerate(moves)]
    for copy in copies:
        copy.start()
    coarse = length // 64
    column = iota((1, width), 1)
    col = lambda n: column + jnp.zeros((n, 1), jnp.int32)
    c1, s1 = phase(iota((coarse, width), 0) * 64, col(coarse), length, False)
    c2, s2 = phase(iota((8, width), 0) * 8, col(8), length, False)
    c3, s3 = phase(iota((8, width), 0), col(8), length, True)
    scale = 1.0 / math.sqrt(length)
    c3, s3 = c3 * scale, s3 * scale
    fine_c = jnp.concatenate([c2[i : i + 1] * c3 - s2[i : i + 1] * s3 for i in range(8)], 0)
    fine_s = jnp.concatenate([s2[i : i + 1] * c3 + c2[i : i + 1] * s3 for i in range(8)], 0)
    for i in range(coarse):
        block = c1[i : i + 1] * fine_c - s1[i : i + 1] * fine_s
        table_ref[64 * i : 64 * i + 64, :] = block.astype(bf16)
    for copy in copies:
        copy.wait()
    marks = marks_of(bins_held, live_held)
    spectra = dot(held_ref[...], table_ref[...]).astype(bf16)
    nothing = jnp.zeros((slots, COLS), bf16)
    for band in range(bands):
        piece = spectra[:, band * COLS : (band + 1) * COLS]
        for tile in range(tiles):
            for t in range(SPAN):
                source = tile - 2 + t
                there = 0 <= source < tiles
                out_ref[tile, band, t * slots : (t + 1) * slots, :] = (
                    piece[source * slots : (source + 1) * slots] if there else nothing
                )
            out_ref[tile, band, SPAN * slots : SPAN * slots + 2, :] = jnp.concatenate(
                [x[tile : tile + 1] for x in marks], 0
            )


def patch_kernel(
    tiles,
    slots,
    arrived_ref,
    probe_ref,
    out_ref,
    st_ref,
    pp_ref,
    own_ref,
    first_ref,
    second_ref,
    sem,
):
    sources = arrived_ref.shape[0]
    per = min(BLOCK_SRC, sources)
    n = per * slots
    chunks = sources // per
    side = chunks + rim_blocks(chunks, n)
    nb = chunks + 2 * side
    pl.run_scoped(
        functools.partial(
            project, slots, arrived_ref, probe_ref, st_ref, pp_ref, own_ref, first_ref, second_ref
        ),
        pltpu.VMEM((nb, COLS, n), f32),
        pltpu.VMEM((nb, 2 * RANK, n), f32),
        pltpu.VMEM((nb, ROWS, n), bf16),
        pltpu.VMEM((nb, n, ROWS), bf16),
        pltpu.VMEM((nb, n, 3 * HC), bf16),
        pltpu.VMEM((SPAN * chunks, 1, n), f32),
        pltpu.VMEM((SPAN * chunks, 8, n), f32),
    )
    pl.run_scoped(
        functools.partial(write, tiles, own_ref, pp_ref, first_ref, second_ref, out_ref, sem),
        pltpu.VMEM((PAIRS, COLS, 2 * HC), f32),
        pltpu.VMEM((OWN_ROWS, HC, COLS), f32),
        pltpu.VMEM((FDEV // JG // 2, 3, 2 * JG * RP, 2 * COLS), bf16),
        pltpu.VMEM((FDEV // JG, 2, 2, RIM, 4 * RP), f32),
    )


def rim_blocks(chunks, n):
    return (min(RIM * HC, chunks * n) + n - 1) // n


def over(chunks, body, carry):
    if chunks == 1:
        return body(0, carry)
    return lax.fori_loop(0, chunks, body, carry)


def project(
    slots,
    arrived_ref,
    probe_ref,
    st_ref,
    pp_ref,
    own_ref,
    first_ref,
    second_ref,
    vt_ref,
    wt_ref,
    ohm_ref,
    ohmt_ref,
    ohht_ref,
    rank_ref,
    fact_ref,
):
    sources = arrived_ref.shape[0]
    per = min(BLOCK_SRC, sources)
    n = per * slots
    chunks = sources // per
    members = ((0, 1), (2,), (3, 4))
    side = chunks + rim_blocks(chunks, n)
    first = (0, side, side + chunks)

    lane_src = (iota((per, n), 1) // slots == iota((per, n), 0)).astype(f32)
    before = (iota((n, n), 0) < iota((n, n), 1)).astype(f32).astype(bf16)

    def locate(chunk, totals):
        totals = list(totals)
        marks = arrived_ref[pl.ds(chunk * per, per), SPAN * slots : SPAN * slots + 2, :].astype(f32)
        facts, used = [], []
        for t in range(SPAN):
            pick = (iota((COLS, n), 0) == t * slots + iota((COLS, n), 1) % slots).astype(f32)
            pick = pick.astype(bf16)
            rows = []
            for i in range(2):
                spread = dot(marks[:, i, :].astype(bf16), pick)
                rows.append(jnp.sum(spread * lane_src, 0, keepdims=True))
            m, h = rows
            good = m < OWN_ROWS
            low, high = m < RIM, good & (m >= OWN_ROWS - RIM)
            keep = (high, good, good, good, low)[t]
            shift = (RIM - OWN_ROWS, RIM, 0, 0, OWN_ROWS)[t]
            inside = (
                (high, None, None),
                (good, high, None),
                (low, good, high),
                (None, low, good),
                (None, None, low),
            )[t]
            fact = [jnp.where(keep, m + shift + 1.0, 0.0), jnp.where(keep, h + 1.0, 0.0)]
            for ok in inside:
                fact.append(jnp.zeros_like(h) if ok is None else jnp.where(ok, h + 1.0, 0.0))
            facts.append(jnp.concatenate(fact + [jnp.zeros((3, n), f32)], 0))
            used.append(keep.astype(f32))
        use = jnp.concatenate(used + [jnp.zeros((8 - SPAN, n), f32)], 0)
        ranks = dot(use.astype(bf16), before)
        sums = jnp.sum(use, 1, keepdims=True)
        for k in range(3):
            for t in members[k]:
                rank = ranks[t : t + 1] + totals[k]
                rank_ref[t * chunks + chunk] = jnp.where(use[t : t + 1] > 0.5, rank, -1.0)
                fact_ref[t * chunks + chunk] = facts[t]
                totals[k] = totals[k] + sums[t : t + 1]
        return tuple(totals)

    zero = jnp.zeros((1, 1), f32)
    totals = over(chunks, locate, (zero, zero, zero))
    counts = [jnp.max(x).astype(jnp.int32) for x in totals]
    filled = [(c + (n - 1)) // n for c in counts]

    p_high, p_low = split(probe_ref[...])

    def pack(k, q):
        def gather(chunk, total, t):
            b = t * chunks + chunk
            wanted = iota((n, n), 0).astype(f32) + (q * n).astype(f32)
            chosen = (wanted == rank_ref[b]).astype(f32).astype(bf16)
            values = arrived_ref[pl.ds(chunk * per, per), t * slots : (t + 1) * slots, :]
            fact = jnp.concatenate([fact_ref[b], jnp.zeros((COLS - 8, n), f32)], 0).T
            both = jnp.concatenate([values.reshape(n, COLS), fact.astype(bf16)], 1)
            part = dot(chosen, both)
            return part if total is None else total + part

        total = None if chunks == 1 else jnp.zeros((n, 2 * COLS), f32)
        for t in members[k]:
            total = over(chunks, functools.partial(gather, t=t), total)
        flip = total.T
        b = first[k] + q
        vt_ref[b] = flip[:COLS]
        row, h = flip[COLS : COLS + 1] - 1.0, flip[COLS + 1 : COLS + 2] - 1.0
        column = total[:, COLS : COLS + 8] - 1.0
        ohm_ref[b] = (iota((ROWS, n), 0).astype(f32) == row).astype(f32).astype(bf16)
        ohmt_ref[b] = (iota((n, ROWS), 1).astype(f32) == column[:, 0:1]).astype(f32).astype(bf16)
        ohht_ref[b] = jnp.concatenate(
            [
                (iota((n, HC), 1).astype(f32) == column[:, 2 + p : 3 + p]).astype(f32)
                for p in range(3)
            ],
            1,
        ).astype(bf16)
        ohh = (iota((HC, n), 0).astype(f32) == h).astype(f32).astype(bf16)
        wt_ref[b] = dot(p_high, ohh) + dot(p_low, ohh)

    for k in range(3):
        pack(k, jnp.int32(0))

    for k in range(3):

        def more(q, carry, k=k):
            pack(k, q)
            return carry

        lax.fori_loop(1, filled[k], more, 0)

    st_ref[:, :, RANK:, :] = jnp.zeros((3, JG, RP - RANK, ROWS), f32)
    pp_ref[:, :, RANK:, :] = jnp.zeros((3, FDEV, RP - RANK, COLS), f32)
    lane = iota((RANK * JG, ROWS), 1)

    def step(g, carry, short, gram_ref, start):
        def sketch_of(b):
            w = wt_ref[b]
            u = []
            for j in range(JG):
                re = vt_ref[b, pl.ds(g * JG + j, 1), :]
                im = vt_ref[b, pl.ds(FDEV + g * JG + j, 1), :]
                u.append(w[:RANK] * re + w[RANK:] * im)
            return dot(jnp.concatenate(u, 0).astype(bf16), ohmt_ref[b])

        def project_of(b, rows):
            at = dot(rows, ohm_ref[b])
            z = []
            for c in range(2):
                for j in range(JG):
                    v = vt_ref[b, pl.ds(c * FDEV + g * JG + j, 1), :]
                    z.append(at[j * RANK : (j + 1) * RANK] * v)
            return dot(jnp.concatenate(z, 0).astype(bf16), ohht_ref[b])

        sketch = [sketch_of(first[k]) for k in range(3)]
        if not short:
            for k in range(3):
                sketch[k] = lax.fori_loop(
                    1, filled[k], lambda q, x, k=k: x + sketch_of(first[k] + q), sketch[k]
                )
        left, own, right = sketch
        sk = [x.astype(bf16) for x in sketch]
        proj = sum(project_of(first[k], sk[k]) for k in range(3))
        if not short:
            for k in range(3):
                proj = lax.fori_loop(
                    1, filled[k], lambda q, x, k=k: x + project_of(first[k] + q, sk[k]), proj
                )
        full_left = jnp.where(lane < ROWS - RIM, left, pltpu.roll(own, ROWS - RIM, 1))
        full_right = jnp.where(lane < ROWS - RIM, right, pltpu.roll(own, ROWS - OWN_ROWS, 1))
        full_own = jnp.where(
            lane < OWN_ROWS,
            own,
            jnp.where(lane < OWN_ROWS + RIM, left, pltpu.roll(right, ROWS - RIM, 1)),
        )
        half = RANK * JG
        re, im = proj[:half], proj[half:]
        lo = iota((half, COLS), 1) < HC
        parts = [
            jnp.where(lo, re[:, :COLS], pltpu.roll(im[:, :COLS], HC, 1)),
            jnp.where(lo, pltpu.roll(re[:, :COLS], HC, 1), im[:, :COLS]),
            jnp.where(
                lo,
                jnp.concatenate([re[:, COLS:], re[:, COLS:]], 1),
                jnp.concatenate([im[:, COLS:], im[:, COLS:]], 1),
            ),
        ]
        for p, whole in enumerate((full_left, full_own, full_right)):
            st_ref[p, :, :RANK, :] = whole.reshape(JG, RANK, ROWS)
            pp_ref[p, pl.ds(g * JG, JG), :RANK, :] = parts[p].reshape(JG, RANK, COLS)
            pad = st_ref[p].reshape(JG * RP, ROWS).astype(bf16)
            if p == 1:
                for q2 in range(2):
                    quad = st_ref[p, 4 * q2 : 4 * q2 + 4].reshape(4 * RP, ROWS)
                    own_ref[2 * g + q2] = quad.T
            gram = lax.dot_general(
                whole.astype(bf16), pad, (((1,), (1,)), ((), ())), preferred_element_type=f32
            )
            for q2 in range(2):
                lanes = iota((RANK, 4 * RP), 1) // RP
                acc = jnp.zeros((RANK, 4 * RP), f32)
                for q in range(4):
                    at = (q2 * 4 + q) * RANK
                    piece = gram[at : at + RANK, q2 * 4 * RP : (q2 + 1) * 4 * RP]
                    acc = jnp.where(lanes == q, piece, acc)
                gram_ref[:, p * (FDEV // 8) + 2 * (g - start) + q2, :] = acc
        return carry

    one_block = jnp.maximum(jnp.maximum(filled[0], filled[1]), filled[2]) <= 1

    steps = FDEV // JG
    half = steps // 2

    @pl.when(one_block)
    def _():
        early = functools.partial(step, short=True, gram_ref=first_ref, start=0)
        lax.fori_loop(0, half, early, 0, unroll=UNROLL)
        work = invert(first_ref)
        for g in range(half, steps):
            for _ in range(PER_STEP):
                next(work, None)
            step(g, 0, True, second_ref, half)
        for _ in work:
            pass

    @pl.when(jnp.logical_not(one_block))
    def _():
        for i, ref in enumerate((first_ref, second_ref)):
            body = functools.partial(step, short=False, gram_ref=ref, start=i * half)
            lax.fori_loop(i * half, (i + 1) * half, body, 0)
        for _ in invert(first_ref):
            pass


def invert(gram_ref):
    wide = 4 * RP
    count = gram_ref.shape[1]
    lane = iota((count, wide), 1) % RP
    base = iota((count, wide), 1) // RP * RP
    same = (iota((wide, wide), 0) // RP == iota((wide, wide), 1) // RP).astype(f32)
    a = [gram_ref[r] for r in range(RANK)]
    diag = jnp.zeros((count, wide), f32)
    for r in range(RANK):
        diag = jnp.where(lane == r, a[r], diag)
    trace = jnp.dot(diag, same, preferred_element_type=f32, precision=lax.Precision.HIGHEST)
    ridge = 0.01 * trace / RANK + 1e-06
    a = [jnp.where(lane == r, a[r] + ridge, a[r]) for r in range(RANK)]
    for k in range(0, RANK, 2):
        c0 = [jnp.take_along_axis(x, base + k, axis=1) for x in a]
        c1 = [jnp.take_along_axis(x, base + (k + 1), axis=1) for x in a]
        x, y, z = c0[k], c1[k], c1[k + 1]
        scale = 1.0 / (x * z - y * y)
        x, y, z = z * scale, -y * scale, x * scale
        n0 = jnp.where(lane == k, x, jnp.where(lane == k + 1, y, x * a[k] + y * a[k + 1]))
        n1 = jnp.where(lane == k, y, jnp.where(lane == k + 1, z, y * a[k] + z * a[k + 1]))
        pair = lane // 2 == k // 2
        for r in range(RANK):
            if r // 2 != k // 2:
                a[r] = jnp.where(pair, 0.0, a[r]) - c0[r] * n0 - c1[r] * n1
        a[k], a[k + 1] = n0, n1
        yield
    for r in range(RANK):
        gram_ref[r] = a[r]


def write(
    tiles,
    own_ref,
    pp_ref,
    first_ref,
    second_ref,
    out_ref,
    sem,
    freq_ref,
    cells_ref,
    weights_ref,
    rim_ref,
):
    count = FDEV // 4
    wide = 4 * RP
    here = lax.axis_index("grid")
    has_left = (here > 0).astype(f32)
    has_right = (here < tiles - 1).astype(f32)
    rim = RIM // 2
    edge = iota((rim * JG, 1), 0) < MY // 2 * JG
    taper_first = jnp.where(edge, 0.6, 0.8)
    taper_last = jnp.where(edge, 0.8, 0.6)
    left_w = jnp.where(edge, 0.4, 0.2) * has_left
    right_w = jnp.where(edge, 0.2, 0.4) * has_right
    lo = iota((wide, COLS), 1) < HC
    mine = [iota((JG, wide), 1) // RP + 4 * q2 == iota((JG, wide), 0) for q2 in range(2)]

    def expand(take, pairs):
        rows = []
        for m in pairs:
            row = []
            for parity in range(2):
                for q2 in range(2):
                    row.append(jnp.where(mine[q2], take(q2, 2 * m + parity), 0.0))
            rows.append(jnp.concatenate(row, 1))
        return jnp.concatenate(rows, 0).astype(bf16)

    def own_rows(g, pairs):
        return expand(lambda q2, m: own_ref[2 * g + q2, pl.ds(m, 1), :], pairs)

    def rim_rows(g, side):
        return expand(lambda q2, m: rim_ref[g, side, q2, pl.ds(m, 1), :], range(rim))

    def weights(g, gram_ref, start):
        w = []
        for p in range(3):
            even, odd = [], []
            for q2 in range(2):
                i = 2 * g + q2
                inverse = gram_ref[:, p * (FDEV // 8) + i - 2 * start, :]
                lanes = iota((RANK, wide), 1) // RP
                zero = jnp.zeros((RP - RANK, wide), f32)
                diag = []
                for q in range(4):
                    diag += [jnp.where(lanes == q, inverse, 0.0), zero]
                b_high, b_low = split(jnp.concatenate(diag, 0))
                c = pp_ref[p, pl.ds(i * 4, 4)].reshape(wide, COLS)
                if p == 1:
                    p_high, p_low = split(c)
                    twice = dot(b_high, jnp.concatenate([p_high, p_low], 1))
                    c = twice[:, :COLS] + twice[:, COLS:] + dot(b_low, p_high)
                else:
                    edge_rows = pl.ds(0 if p == 0 else OWN_ROWS - RIM, RIM)
                    x = own_ref[i, edge_rows, :].astype(bf16)
                    twice = dot(x, jnp.concatenate([b_high, b_low], 1))
                    rim_ref[g, p // 2, q2] = twice[:, :wide] + twice[:, wide:]
                r = pltpu.roll(c, HC, 1)
                even.append(jnp.concatenate([jnp.where(lo, c, 0.0), jnp.where(lo, r, 0.0)], 1))
                odd.append(jnp.concatenate([jnp.where(lo, 0.0, r), jnp.where(lo, 0.0, c)], 1))
            w.append(jnp.concatenate(even + odd, 0).astype(bf16))
        return w

    def put(pairs, g, full):
        for c in range(2):
            part = full[:, c * COLS : (c + 1) * COLS].reshape(len(pairs), JG, COLS)
            at = pl.ds(c * FDEV + g * JG, JG)
            freq_ref[pairs.start : pairs.stop, at, :] = part

    steps = FDEV // JG
    half = steps // 2
    work = invert(second_ref)
    blocks = PAIRS // rim
    for g in range(half):
        for _ in range(PER_STEP):
            next(work, None)
        w = weights(g, first_ref, 0)
        mid = dot(own_rows(g, range(PAIRS)), w[1])
        first, last = rim * JG, (PAIRS - rim) * JG
        begin = mid[:first] * taper_first + dot(rim_rows(g, 0), w[0]) * left_w
        end = mid[last:] * taper_last + dot(rim_rows(g, 1), w[2]) * right_w
        put(range(PAIRS), g, jnp.concatenate([begin, mid[first:last], end], 0))
    for _ in work:
        pass

    def late(g, carry):
        for p, x in enumerate(weights(g, second_ref, half)):
            weights_ref[g - half, p] = x
        return carry

    lax.fori_loop(half, steps, late, 0, unroll=4)
    copies = []
    for b in range(blocks):
        pairs = range(b * rim, (b + 1) * rim)
        for g in range(half, steps):
            part = dot(own_rows(g, pairs), weights_ref[g - half, 1])
            if b == 0:
                part = part * taper_first + dot(rim_rows(g, 0), weights_ref[g - half, 0]) * left_w
            elif b == blocks - 1:
                part = part * taper_last + dot(rim_rows(g, 1), weights_ref[g - half, 2]) * right_w
            put(pairs, g, part)
        for m in pairs:
            cells_ref[2 * m : 2 * m + 2] = freq_ref[m].T.reshape(2, HC, COLS)
        cells = pl.ds(2 * rim * b, 2 * rim)
        copy = pltpu.make_async_copy(cells_ref.at[cells], out_ref.at[cells], sem.at[b])
        copy.start()
        copies.append(copy)
    for copy in copies:
        copy.wait()


def patches(arrived, probe, tiles, slots):
    return pl.pallas_call(
        functools.partial(patch_kernel, tiles, slots),
        out_shape=jax.ShapeDtypeStruct((OWN_ROWS, HC, COLS), f32),
        in_specs=[pl.BlockSpec(memory_space=pltpu.VMEM)] * 2,
        out_specs=pl.BlockSpec(memory_space=pl.ANY),
        scratch_shapes=[
            pltpu.VMEM((3, JG, RP, ROWS), f32),
            pltpu.VMEM((3, FDEV, RP, COLS), f32),
            pltpu.VMEM((FDEV // 4, ROWS, 4 * RP), f32),
            pltpu.VMEM((RANK, 3 * FDEV // 8, 4 * RP), f32),
            pltpu.VMEM((RANK, 3 * FDEV // 8, 4 * RP), f32),
            pltpu.SemaphoreType.DMA((6,)),
        ],
        compiler_params=pltpu.CompilerParams(vmem_limit_bytes=60 * 2**20),
        name="patches",
    )(arrived, probe)


def per_device(traces, bins, live, probe):
    tiles = lax.axis_size("grid")
    bands = lax.axis_size("freq")
    slots, length = traces.shape[2:]
    sources = tiles * bands
    used = SPAN * slots

    vmem = pl.BlockSpec(memory_space=pltpu.VMEM)
    sent = pl.pallas_call(
        spectra_kernel,
        out_shape=jax.ShapeDtypeStruct((tiles, bands, used + 2, COLS), bf16),
        in_specs=[pl.BlockSpec(memory_space=pl.ANY)] * 3,
        out_specs=vmem,
        scratch_shapes=[
            pltpu.VMEM((length, COLS * bands), bf16),
            pltpu.VMEM((tiles * slots, length), bf16),
            pltpu.VMEM((tiles, slots), jnp.int32),
            pltpu.VMEM((tiles, slots), jnp.int32),
            pltpu.SemaphoreType.DMA((3,)),
        ],
        compiler_params=pltpu.CompilerParams(vmem_limit_bytes=60 * 2**20),
        name="spectra",
    )(traces.reshape(tiles * slots, length), bins[0], live[0])

    arrived = lax.all_to_all(
        sent.reshape(sources, used + 2, COLS), ("grid", "freq"), 0, 0, tiled=True
    )

    out = patches(
        arrived, jnp.transpose(probe, (1, 2, 0)).reshape(2 * RANK, HC), tiles, slots
    )
    return out.reshape(OWNX, MY, HC, COLS)


def solution(mesh):
    placed = (
        P(("grid", "freq"), None, None, None),
        P(("grid", "freq"), None, None),
        P(("grid", "freq"), None, None),
        P(),
    )
    return jax.shard_map(
        per_device,
        mesh=mesh,
        in_specs=placed,
        out_specs=P("grid", None, None, "freq"),
        check_vma=False,
    )
```

```python
import functools
import math

import jax
import jax.numpy as jnp
from jax import lax
from jax.experimental import pallas as pl
from jax.experimental.pallas import tpu as pltpu
from jax.sharding import PartitionSpec as P

FDEV = 64
FIRST = 8
PX = 16
MY = 16
HC = 64
MARGIN = 2
OWNX = 12
RANK = 24
SPAN = 5
OWN_ROWS = OWNX * MY
RIM = MARGIN * MY
ROWS = PX * MY
PAIRS = OWN_ROWS // 2
COLS = 2 * FDEV
JG = 8
RP = 32
BLOCK_SRC = 32
DEAD = 255.0
UNROLL = 4
PER_STEP = 3

f32 = jnp.float32
bf16 = jnp.bfloat16


def dot(a, b):
    return jnp.dot(a, b, preferred_element_type=f32)


def split(x):
    high = x.astype(bf16)
    return high, (x - high.astype(f32)).astype(bf16)


def iota(shape, dim):
    return lax.broadcasted_iota(jnp.int32, shape, dim)


def phase(times, columns, length, quarter):
    k = FIRST + columns // COLS * FDEV + columns % FDEV
    turns = ((times * k) & (length - 1)).astype(f32)
    angle = turns * (2.0 * math.pi / length)
    if quarter:
        angle = angle + (columns // FDEV % 2).astype(f32) * (0.5 * math.pi)
    return jnp.cos(angle), jnp.sin(angle)


def marks_of(bins_ref, live_ref):
    tiles, slots = bins_ref.shape
    on = live_ref[...] == 1
    both = jnp.concatenate(
        [
            jnp.where(on, bins_ref[...] // HC, int(DEAD)),
            jnp.where(on, bins_ref[...] % HC, 0),
        ],
        0,
    )
    lanes = iota((slots, SPAN * COLS), 1)
    put = (lanes % COLS == lanes // COLS * slots + iota((slots, SPAN * COLS), 0)).astype(f32)
    placed = dot(both.astype(f32).astype(bf16), put.astype(bf16))
    tile, lane = iota((tiles, COLS), 0), iota((tiles, COLS), 1)
    marks = []
    for i, other in enumerate((DEAD, 0.0)):
        mark = jnp.full((tiles, COLS), other, f32)
        for t in range(SPAN):
            moved = placed[i * tiles : (i + 1) * tiles, t * COLS : (t + 1) * COLS]
            if t != 2:
                moved = pltpu.roll(moved, (2 - t) % tiles, 0)
            there = (tile + (t - 2) >= 0) & (tile + (t - 2) < tiles) & (lane // slots == t)
            mark = jnp.where(there, moved, mark)
        marks.append(mark.astype(bf16))
    return marks


def spectra_kernel(
    traces_ref, bins_ref, live_ref, out_ref, table_ref, held_ref, bins_held, live_held, sem
):
    length, width = table_ref.shape
    tiles, bands = out_ref.shape[:2]
    slots = bins_ref.shape[1]
    moves = ((bins_ref, bins_held), (live_ref, live_held), (traces_ref, held_ref))
    copies = [pltpu.make_async_copy(a, b, sem.at[i]) for i, (a, b) in enumerate(moves)]
    for copy in copies:
        copy.start()
    coarse = length // 64
    column = iota((1, width), 1)
    col = lambda n: column + jnp.zeros((n, 1), jnp.int32)
    c1, s1 = phase(iota((coarse, width), 0) * 64, col(coarse), length, False)
    c2, s2 = phase(iota((8, width), 0) * 8, col(8), length, False)
    c3, s3 = phase(iota((8, width), 0), col(8), length, True)
    scale = 1.0 / math.sqrt(length)
    c3, s3 = c3 * scale, s3 * scale
    fine_c = jnp.concatenate([c2[i : i + 1] * c3 - s2[i : i + 1] * s3 for i in range(8)], 0)
    fine_s = jnp.concatenate([s2[i : i + 1] * c3 + c2[i : i + 1] * s3 for i in range(8)], 0)
    for i in range(coarse):
        block = c1[i : i + 1] * fine_c - s1[i : i + 1] * fine_s
        table_ref[64 * i : 64 * i + 64, :] = block.astype(bf16)
    for copy in copies:
        copy.wait()
    marks = marks_of(bins_held, live_held)
    spectra = dot(held_ref[...], table_ref[...]).astype(bf16)
    nothing = jnp.zeros((slots, COLS), bf16)
    for band in range(bands):
        piece = spectra[:, band * COLS : (band + 1) * COLS]
        for tile in range(tiles):
            for t in range(SPAN):
                source = tile - 2 + t
                there = 0 <= source < tiles
                out_ref[tile, band, t * slots : (t + 1) * slots, :] = (
                    piece[source * slots : (source + 1) * slots] if there else nothing
                )
            out_ref[tile, band, SPAN * slots : SPAN * slots + 2, :] = jnp.concatenate(
                [x[tile : tile + 1] for x in marks], 0
            )


def patch_kernel(
    tiles,
    slots,
    arrived_ref,
    probe_ref,
    out_ref,
    st_ref,
    pp_ref,
    own_ref,
    first_ref,
    second_ref,
    sem,
):
    sources = arrived_ref.shape[0]
    per = min(BLOCK_SRC, sources)
    n = per * slots
    chunks = sources // per
    side = chunks + rim_blocks(chunks, n)
    nb = chunks + 2 * side
    pl.run_scoped(
        functools.partial(
            project, slots, arrived_ref, probe_ref, st_ref, pp_ref, own_ref, first_ref, second_ref
        ),
        pltpu.VMEM((nb, COLS, n), f32),
        pltpu.VMEM((nb, 2 * RANK, n), f32),
        pltpu.VMEM((nb, ROWS, n), bf16),
        pltpu.VMEM((nb, n, ROWS), bf16),
        pltpu.VMEM((nb, n, 3 * HC), bf16),
        pltpu.VMEM((SPAN * chunks, 1, n), f32),
        pltpu.VMEM((SPAN * chunks, 8, n), f32),
    )
    pl.run_scoped(
        functools.partial(write, tiles, own_ref, pp_ref, first_ref, second_ref, out_ref, sem),
        pltpu.VMEM((PAIRS, COLS, 2 * HC), f32),
        pltpu.VMEM((OWN_ROWS, HC, COLS), f32),
        pltpu.VMEM((FDEV // JG // 2, 3, 2 * JG * RP, 2 * COLS), bf16),
        pltpu.VMEM((FDEV // JG, 2, 2, RIM, 4 * RP), f32),
    )


def rim_blocks(chunks, n):
    return (min(RIM * HC, chunks * n) + n - 1) // n


def over(chunks, body, carry):
    if chunks == 1:
        return body(0, carry)
    return lax.fori_loop(0, chunks, body, carry)


def project(
    slots,
    arrived_ref,
    probe_ref,
    st_ref,
    pp_ref,
    own_ref,
    first_ref,
    second_ref,
    vt_ref,
    wt_ref,
    ohm_ref,
    ohmt_ref,
    ohht_ref,
    rank_ref,
    fact_ref,
):
    sources = arrived_ref.shape[0]
    per = min(BLOCK_SRC, sources)
    n = per * slots
    chunks = sources // per
    main, rim_tile = (1, 2, 3), (0, None, 4)
    side = chunks + rim_blocks(chunks, n)
    first = (0, side, side + chunks)

    lane_src = (iota((per, n), 1) // slots == iota((per, n), 0)).astype(f32)
    before = (iota((n, n), 0) < iota((n, n), 1)).astype(f32).astype(bf16)

    def locate(chunk, totals):
        totals = list(totals)
        marks = arrived_ref[pl.ds(chunk * per, per), SPAN * slots : SPAN * slots + 2, :].astype(f32)
        facts, used = [], []
        for t in range(SPAN):
            pick = (iota((COLS, n), 0) == t * slots + iota((COLS, n), 1) % slots).astype(f32)
            pick = pick.astype(bf16)
            rows = []
            for i in range(2):
                spread = dot(marks[:, i, :].astype(bf16), pick)
                rows.append(jnp.sum(spread * lane_src, 0, keepdims=True))
            m, h = rows
            good = m < OWN_ROWS
            low, high = m < RIM, good & (m >= OWN_ROWS - RIM)
            keep = (high, good, good, good, low)[t]
            shift = (RIM - OWN_ROWS, RIM, 0, 0, OWN_ROWS)[t]
            inside = (
                (high, None, None),
                (good, high, None),
                (low, good, high),
                (None, low, good),
                (None, None, low),
            )[t]
            fact = [jnp.where(keep, m + shift + 1.0, 0.0), jnp.where(keep, h + 1.0, 0.0)]
            for ok in inside:
                fact.append(jnp.zeros_like(h) if ok is None else jnp.where(ok, h + 1.0, 0.0))
            facts.append(fact)
            used.append(keep.astype(f32))
        free = [1.0 - used[1], 1.0 - used[3]]
        use = jnp.concatenate(used + free + [jnp.zeros((1, n), f32)], 0)
        ranks = dot(use.astype(bf16), before)
        sums = jnp.sum(use, 1, keepdims=True)
        for t in range(SPAN):
            seat = jnp.zeros((1, n), f32)
            if t in (1, 3):
                i = SPAN + t // 2
                seat = jnp.where(use[i : i + 1] > 0.5, ranks[i : i + 1], -2.0)
            fact_ref[t * chunks + chunk] = jnp.concatenate(
                facts[t] + [jnp.zeros((2, n), f32), seat], 0
            )
        for i, t in enumerate((0, 4)):
            rank = ranks[t : t + 1] + totals[i]
            rank_ref[t * chunks + chunk] = jnp.where(use[t : t + 1] > 0.5, rank, -1.0)
            totals[i] = totals[i] + sums[t : t + 1]
            totals[2 + i] = totals[2 + i] + sums[SPAN + i : SPAN + i + 1]
        return tuple(totals)

    zero = jnp.zeros((1, 1), f32)
    totals = over(chunks, locate, (zero,) * 4)
    seated = totals[2:] if chunks == 1 else (zero, zero)
    left_over = [
        jnp.max(jnp.maximum(x - y, 0.0)).astype(jnp.int32) for x, y in zip(totals[:2], seated)
    ]
    filled = [
        chunks + (left_over[0] + (n - 1)) // n,
        chunks,
        chunks + (left_over[1] + (n - 1)) // n,
    ]

    p_high, p_low = split(probe_ref[...])

    def contents(t, chunk):
        values = arrived_ref[pl.ds(chunk * per, per), t * slots : (t + 1) * slots, :]
        fact = jnp.concatenate([fact_ref[t * chunks + chunk], jnp.zeros((COLS - 8, n), f32)], 0)
        return values.reshape(n, COLS), fact.T

    def moved(chosen, t, chunk):
        values, fact = contents(t, chunk)
        both = jnp.concatenate([values, fact.astype(bf16)], 1)
        return dot(chosen.astype(f32).astype(bf16), both)

    def direct(k, chunk):
        values, fact = contents(main[k], chunk)
        total = jnp.concatenate([values.astype(f32), fact], 1)
        if chunks == 1 and k != 1:
            guest = moved(fact[:, 7:8] == rank_ref[rim_tile[k]], rim_tile[k], 0)
            total = jnp.where(fact[:, 0:1] > 0.0, total, guest)
        finish(first[k] + chunk, total)

    def extra(k, q):
        wanted = iota((n, n), 0).astype(f32) + ((q - chunks) * n).astype(f32) + seated[k // 2]

        def gather(chunk, total):
            t = rim_tile[k]
            part = moved(wanted == rank_ref[t * chunks + chunk], t, chunk)
            return part if total is None else total + part

        total = None if chunks == 1 else jnp.zeros((n, 2 * COLS), f32)
        finish(first[k] + q, over(chunks, gather, total))

    def finish(b, total):
        flip = total.T
        vt_ref[b] = flip[:COLS]
        row, h = flip[COLS : COLS + 1] - 1.0, flip[COLS + 1 : COLS + 2] - 1.0
        column = total[:, COLS : COLS + 8] - 1.0
        ohm_ref[b] = (iota((ROWS, n), 0).astype(f32) == row).astype(f32).astype(bf16)
        ohmt_ref[b] = (iota((n, ROWS), 1).astype(f32) == column[:, 0:1]).astype(f32).astype(bf16)
        ohht_ref[b] = jnp.concatenate(
            [
                (iota((n, HC), 1).astype(f32) == column[:, 2 + p : 3 + p]).astype(f32)
                for p in range(3)
            ],
            1,
        ).astype(bf16)
        ohh = (iota((HC, n), 0).astype(f32) == h).astype(f32).astype(bf16)
        wt_ref[b] = dot(p_high, ohh) + dot(p_low, ohh)

    for k in range(3):

        def place(chunk, carry, k=k):
            direct(k, chunk)
            return carry

        over(chunks, place, 0)

    one_block = jnp.maximum(filled[0], filled[2]) <= 1

    @pl.when(jnp.logical_not(one_block))
    def _():
        for k in (0, 2):

            def more(q, carry, k=k):
                extra(k, q)
                return carry

            lax.fori_loop(chunks, filled[k], more, 0)

    st_ref[:, :, RANK:, :] = jnp.zeros((3, JG, RP - RANK, ROWS), f32)
    pp_ref[:, :, RANK:, :] = jnp.zeros((3, FDEV, RP - RANK, COLS), f32)
    lane = iota((RANK * JG, ROWS), 1)

    def step(g, carry, short, gram_ref, start):
        def sketch_of(b):
            w = wt_ref[b]
            u = []
            for j in range(JG):
                re = vt_ref[b, pl.ds(g * JG + j, 1), :]
                im = vt_ref[b, pl.ds(FDEV + g * JG + j, 1), :]
                u.append(w[:RANK] * re + w[RANK:] * im)
            return dot(jnp.concatenate(u, 0).astype(bf16), ohmt_ref[b])

        def project_of(b, rows):
            at = dot(rows, ohm_ref[b])
            z = []
            for c in range(2):
                for j in range(JG):
                    v = vt_ref[b, pl.ds(c * FDEV + g * JG + j, 1), :]
                    z.append(at[j * RANK : (j + 1) * RANK] * v)
            return dot(jnp.concatenate(z, 0).astype(bf16), ohht_ref[b])

        sketch = [sketch_of(first[k]) for k in range(3)]
        if not short:
            for k in range(3):
                sketch[k] = lax.fori_loop(
                    1, filled[k], lambda q, x, k=k: x + sketch_of(first[k] + q), sketch[k]
                )
        left, own, right = sketch
        sk = [x.astype(bf16) for x in sketch]
        proj = sum(project_of(first[k], sk[k]) for k in range(3))
        if not short:
            for k in range(3):
                proj = lax.fori_loop(
                    1, filled[k], lambda q, x, k=k: x + project_of(first[k] + q, sk[k]), proj
                )
        full_left = jnp.where(lane < ROWS - RIM, left, pltpu.roll(own, ROWS - RIM, 1))
        full_right = jnp.where(lane < ROWS - RIM, right, pltpu.roll(own, ROWS - OWN_ROWS, 1))
        full_own = jnp.where(
            lane < OWN_ROWS,
            own,
            jnp.where(lane < OWN_ROWS + RIM, left, pltpu.roll(right, ROWS - RIM, 1)),
        )
        half = RANK * JG
        re, im = proj[:half], proj[half:]
        lo = iota((half, COLS), 1) < HC
        parts = [
            jnp.where(lo, re[:, :COLS], pltpu.roll(im[:, :COLS], HC, 1)),
            jnp.where(lo, pltpu.roll(re[:, :COLS], HC, 1), im[:, :COLS]),
            jnp.where(
                lo,
                jnp.concatenate([re[:, COLS:], re[:, COLS:]], 1),
                jnp.concatenate([im[:, COLS:], im[:, COLS:]], 1),
            ),
        ]
        for p, whole in enumerate((full_left, full_own, full_right)):
            st_ref[p, :, :RANK, :] = whole.reshape(JG, RANK, ROWS)
            pp_ref[p, pl.ds(g * JG, JG), :RANK, :] = parts[p].reshape(JG, RANK, COLS)
            pad = st_ref[p].reshape(JG * RP, ROWS).astype(bf16)
            if p == 1:
                for q2 in range(2):
                    quad = st_ref[p, 4 * q2 : 4 * q2 + 4].reshape(4 * RP, ROWS)
                    own_ref[2 * g + q2] = quad.T
            gram = lax.dot_general(
                whole.astype(bf16), pad, (((1,), (1,)), ((), ())), preferred_element_type=f32
            )
            for q2 in range(2):
                lanes = iota((RANK, 4 * RP), 1) // RP
                acc = jnp.zeros((RANK, 4 * RP), f32)
                for q in range(4):
                    at = (q2 * 4 + q) * RANK
                    piece = gram[at : at + RANK, q2 * 4 * RP : (q2 + 1) * 4 * RP]
                    acc = jnp.where(lanes == q, piece, acc)
                gram_ref[:, p * (FDEV // 8) + 2 * (g - start) + q2, :] = acc
        return carry


    steps = FDEV // JG
    half = steps // 2

    @pl.when(one_block)
    def _():
        early = functools.partial(step, short=True, gram_ref=first_ref, start=0)
        lax.fori_loop(0, half, early, 0, unroll=UNROLL)
        work = invert(first_ref)
        for g in range(half, steps):
            for _ in range(PER_STEP):
                next(work, None)
            step(g, 0, True, second_ref, half)
        for _ in work:
            pass

    @pl.when(jnp.logical_not(one_block))
    def _():
        for i, ref in enumerate((first_ref, second_ref)):
            body = functools.partial(step, short=False, gram_ref=ref, start=i * half)
            lax.fori_loop(i * half, (i + 1) * half, body, 0)
        for _ in invert(first_ref):
            pass


def invert(gram_ref):
    wide = 4 * RP
    count = gram_ref.shape[1]
    lane = iota((count, wide), 1) % RP
    base = iota((count, wide), 1) // RP * RP
    same = (iota((wide, wide), 0) // RP == iota((wide, wide), 1) // RP).astype(f32)
    a = [gram_ref[r] for r in range(RANK)]
    diag = jnp.zeros((count, wide), f32)
    for r in range(RANK):
        diag = jnp.where(lane == r, a[r], diag)
    trace = jnp.dot(diag, same, preferred_element_type=f32, precision=lax.Precision.HIGHEST)
    ridge = 0.01 * trace / RANK + 1e-06
    a = [jnp.where(lane == r, a[r] + ridge, a[r]) for r in range(RANK)]
    for k in range(0, RANK, 2):
        c0 = [jnp.take_along_axis(x, base + k, axis=1) for x in a]
        c1 = [jnp.take_along_axis(x, base + (k + 1), axis=1) for x in a]
        x, y, z = c0[k], c1[k], c1[k + 1]
        scale = 1.0 / (x * z - y * y)
        x, y, z = z * scale, -y * scale, x * scale
        n0 = jnp.where(lane == k, x, jnp.where(lane == k + 1, y, x * a[k] + y * a[k + 1]))
        n1 = jnp.where(lane == k, y, jnp.where(lane == k + 1, z, y * a[k] + z * a[k + 1]))
        pair = lane // 2 == k // 2
        for r in range(RANK):
            if r // 2 != k // 2:
                a[r] = jnp.where(pair, 0.0, a[r]) - c0[r] * n0 - c1[r] * n1
        a[k], a[k + 1] = n0, n1
        yield
    for r in range(RANK):
        gram_ref[r] = a[r]


def write(
    tiles,
    own_ref,
    pp_ref,
    first_ref,
    second_ref,
    out_ref,
    sem,
    freq_ref,
    cells_ref,
    weights_ref,
    rim_ref,
):
    count = FDEV // 4
    wide = 4 * RP
    here = lax.axis_index("grid")
    has_left = (here > 0).astype(f32)
    has_right = (here < tiles - 1).astype(f32)
    rim = RIM // 2
    edge = iota((rim * JG, 1), 0) < MY // 2 * JG
    taper_first = jnp.where(edge, 0.6, 0.8)
    taper_last = jnp.where(edge, 0.8, 0.6)
    left_w = jnp.where(edge, 0.4, 0.2) * has_left
    right_w = jnp.where(edge, 0.2, 0.4) * has_right
    lo = iota((wide, COLS), 1) < HC
    mine = [iota((JG, wide), 1) // RP + 4 * q2 == iota((JG, wide), 0) for q2 in range(2)]

    def expand(take, pairs):
        rows = []
        for m in pairs:
            row = []
            for parity in range(2):
                for q2 in range(2):
                    row.append(jnp.where(mine[q2], take(q2, 2 * m + parity), 0.0))
            rows.append(jnp.concatenate(row, 1))
        return jnp.concatenate(rows, 0).astype(bf16)

    def own_rows(g, pairs):
        return expand(lambda q2, m: own_ref[2 * g + q2, pl.ds(m, 1), :], pairs)

    def rim_rows(g, side):
        return expand(lambda q2, m: rim_ref[g, side, q2, pl.ds(m, 1), :], range(rim))

    def weights(g, gram_ref, start):
        w = []
        for p in range(3):
            even, odd = [], []
            for q2 in range(2):
                i = 2 * g + q2
                inverse = gram_ref[:, p * (FDEV // 8) + i - 2 * start, :]
                lanes = iota((RANK, wide), 1) // RP
                zero = jnp.zeros((RP - RANK, wide), f32)
                diag = []
                for q in range(4):
                    diag += [jnp.where(lanes == q, inverse, 0.0), zero]
                b_high, b_low = split(jnp.concatenate(diag, 0))
                c = pp_ref[p, pl.ds(i * 4, 4)].reshape(wide, COLS)
                if p == 1:
                    p_high, p_low = split(c)
                    twice = dot(b_high, jnp.concatenate([p_high, p_low], 1))
                    c = twice[:, :COLS] + twice[:, COLS:] + dot(b_low, p_high)
                else:
                    edge_rows = pl.ds(0 if p == 0 else OWN_ROWS - RIM, RIM)
                    x = own_ref[i, edge_rows, :].astype(bf16)
                    twice = dot(x, jnp.concatenate([b_high, b_low], 1))
                    rim_ref[g, p // 2, q2] = twice[:, :wide] + twice[:, wide:]
                r = pltpu.roll(c, HC, 1)
                even.append(jnp.concatenate([jnp.where(lo, c, 0.0), jnp.where(lo, r, 0.0)], 1))
                odd.append(jnp.concatenate([jnp.where(lo, 0.0, r), jnp.where(lo, 0.0, c)], 1))
            w.append(jnp.concatenate(even + odd, 0).astype(bf16))
        return w

    def put(pairs, g, full):
        for c in range(2):
            part = full[:, c * COLS : (c + 1) * COLS].reshape(len(pairs), JG, COLS)
            at = pl.ds(c * FDEV + g * JG, JG)
            freq_ref[pairs.start : pairs.stop, at, :] = part

    steps = FDEV // JG
    half = steps // 2
    work = invert(second_ref)
    blocks = PAIRS // rim
    for g in range(half):
        for _ in range(PER_STEP):
            next(work, None)
        w = weights(g, first_ref, 0)
        mid = dot(own_rows(g, range(PAIRS)), w[1])
        first, last = rim * JG, (PAIRS - rim) * JG
        begin = mid[:first] * taper_first + dot(rim_rows(g, 0), w[0]) * left_w
        end = mid[last:] * taper_last + dot(rim_rows(g, 1), w[2]) * right_w
        put(range(PAIRS), g, jnp.concatenate([begin, mid[first:last], end], 0))
    for _ in work:
        pass

    def late(g, carry):
        for p, x in enumerate(weights(g, second_ref, half)):
            weights_ref[g - half, p] = x
        return carry

    lax.fori_loop(half, steps, late, 0, unroll=4)
    copies = []
    for b in range(blocks):
        pairs = range(b * rim, (b + 1) * rim)
        for g in range(half, steps):
            part = dot(own_rows(g, pairs), weights_ref[g - half, 1])
            if b == 0:
                part = part * taper_first + dot(rim_rows(g, 0), weights_ref[g - half, 0]) * left_w
            elif b == blocks - 1:
                part = part * taper_last + dot(rim_rows(g, 1), weights_ref[g - half, 2]) * right_w
            put(pairs, g, part)
        for m in pairs:
            cells_ref[2 * m : 2 * m + 2] = freq_ref[m].T.reshape(2, HC, COLS)
        cells = pl.ds(2 * rim * b, 2 * rim)
        copy = pltpu.make_async_copy(cells_ref.at[cells], out_ref.at[cells], sem.at[b])
        copy.start()
        copies.append(copy)
    for copy in copies:
        copy.wait()


def patches(arrived, probe, tiles, slots):
    return pl.pallas_call(
        functools.partial(patch_kernel, tiles, slots),
        out_shape=jax.ShapeDtypeStruct((OWN_ROWS, HC, COLS), f32),
        in_specs=[pl.BlockSpec(memory_space=pltpu.VMEM)] * 2,
        out_specs=pl.BlockSpec(memory_space=pl.ANY),
        scratch_shapes=[
            pltpu.VMEM((3, JG, RP, ROWS), f32),
            pltpu.VMEM((3, FDEV, RP, COLS), f32),
            pltpu.VMEM((FDEV // 4, ROWS, 4 * RP), f32),
            pltpu.VMEM((RANK, 3 * FDEV // 8, 4 * RP), f32),
            pltpu.VMEM((RANK, 3 * FDEV // 8, 4 * RP), f32),
            pltpu.SemaphoreType.DMA((6,)),
        ],
        compiler_params=pltpu.CompilerParams(vmem_limit_bytes=60 * 2**20),
        name="patches",
    )(arrived, probe)


def per_device(traces, bins, live, probe):
    tiles = lax.axis_size("grid")
    bands = lax.axis_size("freq")
    slots, length = traces.shape[2:]
    sources = tiles * bands
    used = SPAN * slots

    vmem = pl.BlockSpec(memory_space=pltpu.VMEM)
    sent = pl.pallas_call(
        spectra_kernel,
        out_shape=jax.ShapeDtypeStruct((tiles, bands, used + 2, COLS), bf16),
        in_specs=[pl.BlockSpec(memory_space=pl.ANY)] * 3,
        out_specs=vmem,
        scratch_shapes=[
            pltpu.VMEM((length, COLS * bands), bf16),
            pltpu.VMEM((tiles * slots, length), bf16),
            pltpu.VMEM((tiles, slots), jnp.int32),
            pltpu.VMEM((tiles, slots), jnp.int32),
            pltpu.SemaphoreType.DMA((3,)),
        ],
        compiler_params=pltpu.CompilerParams(vmem_limit_bytes=60 * 2**20),
        name="spectra",
    )(traces.reshape(tiles * slots, length), bins[0], live[0])

    arrived = lax.all_to_all(
        sent.reshape(sources, used + 2, COLS), ("grid", "freq"), 0, 0, tiled=True
    )

    out = patches(
        arrived, jnp.transpose(probe, (1, 2, 0)).reshape(2 * RANK, HC), tiles, slots
    )
    return out.reshape(OWNX, MY, HC, COLS)


def solution(mesh):
    placed = (
        P(("grid", "freq"), None, None, None),
        P(("grid", "freq"), None, None),
        P(("grid", "freq"), None, None),
        P(),
    )
    return jax.shard_map(
        per_device,
        mesh=mesh,
        in_specs=placed,
        out_specs=P("grid", None, None, "freq"),
        check_vma=False,
    )
```

```python
import functools
import math

import jax
import jax.numpy as jnp
from jax import lax
from jax.experimental import pallas as pl
from jax.experimental.pallas import tpu as pltpu
from jax.sharding import PartitionSpec as P

FDEV = 64
FIRST = 8
PX = 16
MY = 16
HC = 64
MARGIN = 2
OWNX = 12
RANK = 24
SPAN = 5
OWN_ROWS = OWNX * MY
RIM = MARGIN * MY
ROWS = PX * MY
PAIRS = OWN_ROWS // 2
COLS = 2 * FDEV
JG = 8
RP = 32
BLOCK_SRC = 32
DEAD = 255.0
UNROLL = 4
PER_STEP = 3

f32 = jnp.float32
bf16 = jnp.bfloat16


def dot(a, b):
    return jnp.dot(a, b, preferred_element_type=f32)


def split(x):
    high = x.astype(bf16)
    return high, (x - high.astype(f32)).astype(bf16)


def iota(shape, dim):
    return lax.broadcasted_iota(jnp.int32, shape, dim)


def phase(times, columns, length, quarter):
    k = FIRST + columns // COLS * FDEV + columns % FDEV
    turns = ((times * k) & (length - 1)).astype(f32)
    angle = turns * (2.0 * math.pi / length)
    if quarter:
        angle = angle + (columns // FDEV % 2).astype(f32) * (0.5 * math.pi)
    return jnp.cos(angle), jnp.sin(angle)


def marks_of(bins_ref, live_ref):
    tiles, slots = bins_ref.shape
    on = live_ref[...] == 1
    both = jnp.concatenate(
        [
            jnp.where(on, bins_ref[...] // HC, int(DEAD)),
            jnp.where(on, bins_ref[...] % HC, 0),
        ],
        0,
    )
    lanes = iota((slots, SPAN * COLS), 1)
    put = (lanes % COLS == lanes // COLS * slots + iota((slots, SPAN * COLS), 0)).astype(f32)
    placed = dot(both.astype(f32).astype(bf16), put.astype(bf16))
    tile, lane = iota((tiles, COLS), 0), iota((tiles, COLS), 1)
    marks = []
    for i, other in enumerate((DEAD, 0.0)):
        mark = jnp.full((tiles, COLS), other, f32)
        for t in range(SPAN):
            moved = placed[i * tiles : (i + 1) * tiles, t * COLS : (t + 1) * COLS]
            if t != 2:
                moved = pltpu.roll(moved, (2 - t) % tiles, 0)
            there = (tile + (t - 2) >= 0) & (tile + (t - 2) < tiles) & (lane // slots == t)
            mark = jnp.where(there, moved, mark)
        marks.append(mark.astype(bf16))
    return marks


def spectra_kernel(
    traces_ref, bins_ref, live_ref, out_ref, table_ref, held_ref, bins_held, live_held, sem
):
    length, width = table_ref.shape
    tiles, bands = out_ref.shape[:2]
    slots = bins_ref.shape[1]
    moves = ((bins_ref, bins_held), (live_ref, live_held), (traces_ref, held_ref))
    copies = [pltpu.make_async_copy(a, b, sem.at[i]) for i, (a, b) in enumerate(moves)]
    for copy in copies:
        copy.start()
    coarse = length // 64
    column = iota((1, width), 1)
    col = lambda n: column + jnp.zeros((n, 1), jnp.int32)
    c1, s1 = phase(iota((coarse, width), 0) * 64, col(coarse), length, False)
    c2, s2 = phase(iota((8, width), 0) * 8, col(8), length, False)
    c3, s3 = phase(iota((8, width), 0), col(8), length, True)
    scale = 1.0 / math.sqrt(length)
    c3, s3 = c3 * scale, s3 * scale
    fine_c = jnp.concatenate([c2[i : i + 1] * c3 - s2[i : i + 1] * s3 for i in range(8)], 0)
    fine_s = jnp.concatenate([s2[i : i + 1] * c3 + c2[i : i + 1] * s3 for i in range(8)], 0)
    for i in range(coarse):
        block = c1[i : i + 1] * fine_c - s1[i : i + 1] * fine_s
        table_ref[64 * i : 64 * i + 64, :] = block.astype(bf16)
    for copy in copies:
        copy.wait()
    marks = marks_of(bins_held, live_held)
    spectra = dot(held_ref[...], table_ref[...]).astype(bf16)
    nothing = jnp.zeros((slots, COLS), bf16)
    for band in range(bands):
        piece = spectra[:, band * COLS : (band + 1) * COLS]
        for tile in range(tiles):
            for t in range(SPAN):
                source = tile - 2 + t
                there = 0 <= source < tiles
                out_ref[tile, band, t * slots : (t + 1) * slots, :] = (
                    piece[source * slots : (source + 1) * slots] if there else nothing
                )
            out_ref[tile, band, SPAN * slots : SPAN * slots + 2, :] = jnp.concatenate(
                [x[tile : tile + 1] for x in marks], 0
            )


def patch_kernel(
    tiles,
    slots,
    arrived_ref,
    probe_ref,
    out_ref,
    st_ref,
    pp_ref,
    own_ref,
    first_ref,
    second_ref,
    sem,
):
    sources = arrived_ref.shape[0]
    per = min(BLOCK_SRC, sources)
    n = per * slots
    chunks = sources // per
    side = chunks + rim_blocks(chunks, n)
    nb = chunks + 2 * side
    pl.run_scoped(
        functools.partial(
            project, slots, arrived_ref, probe_ref, st_ref, pp_ref, own_ref, first_ref, second_ref
        ),
        pltpu.VMEM((nb, COLS, n), f32),
        pltpu.VMEM((nb, 2 * RANK, n), f32),
        pltpu.VMEM((nb, ROWS, n), bf16),
        pltpu.VMEM((nb, n, ROWS), bf16),
        pltpu.VMEM((nb, n, 3 * HC), bf16),
        pltpu.VMEM((SPAN * chunks, 1, n), f32),
        pltpu.VMEM((SPAN * chunks, 8, n), f32),
    )
    pl.run_scoped(
        functools.partial(write, tiles, own_ref, pp_ref, first_ref, second_ref, out_ref, sem),
        pltpu.VMEM((PAIRS, COLS, 2 * HC), f32),
        pltpu.VMEM((OWN_ROWS, HC, COLS), f32),
        pltpu.VMEM((FDEV // JG // 2, 3, 2 * JG * RP, 2 * COLS), bf16),
        pltpu.VMEM((FDEV // JG, 2, 2, RIM, 4 * RP), f32),
    )


def rim_blocks(chunks, n):
    return (min(RIM * HC, chunks * n) + n - 1) // n


def over(chunks, body, carry):
    if chunks == 1:
        return body(0, carry)
    return lax.fori_loop(0, chunks, body, carry)


def project(
    slots,
    arrived_ref,
    probe_ref,
    st_ref,
    pp_ref,
    own_ref,
    first_ref,
    second_ref,
    vt_ref,
    wt_ref,
    ohm_ref,
    ohmt_ref,
    ohht_ref,
    rank_ref,
    fact_ref,
):
    sources = arrived_ref.shape[0]
    per = min(BLOCK_SRC, sources)
    n = per * slots
    chunks = sources // per
    main, rim_tile = (1, 2, 3), (0, None, 4)
    side = chunks + rim_blocks(chunks, n)
    first = (0, side, side + chunks)

    lane_src = (iota((per, n), 1) // slots == iota((per, n), 0)).astype(f32)
    before = (iota((n, n), 0) < iota((n, n), 1)).astype(f32).astype(bf16)

    def locate(chunk, totals):
        totals = list(totals)
        marks = arrived_ref[pl.ds(chunk * per, per), SPAN * slots : SPAN * slots + 2, :].astype(f32)
        facts, used = [], []
        for t in range(SPAN):
            pick = (iota((COLS, n), 0) == t * slots + iota((COLS, n), 1) % slots).astype(f32)
            pick = pick.astype(bf16)
            rows = []
            for i in range(2):
                spread = dot(marks[:, i, :].astype(bf16), pick)
                rows.append(jnp.sum(spread * lane_src, 0, keepdims=True))
            m, h = rows
            good = m < OWN_ROWS
            low, high = m < RIM, good & (m >= OWN_ROWS - RIM)
            keep = (high, good, good, good, low)[t]
            shift = (RIM - OWN_ROWS, RIM, 0, 0, OWN_ROWS)[t]
            inside = (
                (high, None, None),
                (good, high, None),
                (low, good, high),
                (None, low, good),
                (None, None, low),
            )[t]
            fact = [jnp.where(keep, m + shift + 1.0, 0.0), jnp.where(keep, h + 1.0, 0.0)]
            for ok in inside:
                fact.append(jnp.zeros_like(h) if ok is None else jnp.where(ok, h + 1.0, 0.0))
            facts.append(fact)
            used.append(keep.astype(f32))
        free = [1.0 - used[1], 1.0 - used[3]]
        use = jnp.concatenate(used + free + [jnp.zeros((1, n), f32)], 0)
        ranks = dot(use.astype(bf16), before)
        sums = jnp.sum(use, 1, keepdims=True)
        for t in range(SPAN):
            seat = jnp.zeros((1, n), f32)
            if t in (1, 3):
                i = SPAN + t // 2
                seat = jnp.where(use[i : i + 1] > 0.5, ranks[i : i + 1], -2.0)
            fact_ref[t * chunks + chunk] = jnp.concatenate(
                facts[t] + [jnp.zeros((2, n), f32), seat], 0
            )
        for i, t in enumerate((0, 4)):
            rank = ranks[t : t + 1] + totals[i]
            rank_ref[t * chunks + chunk] = jnp.where(use[t : t + 1] > 0.5, rank, -1.0)
            totals[i] = totals[i] + sums[t : t + 1]
            totals[2 + i] = totals[2 + i] + sums[SPAN + i : SPAN + i + 1]
        return tuple(totals)

    zero = jnp.zeros((1, 1), f32)
    totals = over(chunks, locate, (zero,) * 4)
    seated = totals[2:] if chunks == 1 else (zero, zero)
    left_over = [
        jnp.max(jnp.maximum(x - y, 0.0)).astype(jnp.int32) for x, y in zip(totals[:2], seated)
    ]
    filled = [
        chunks + (left_over[0] + (n - 1)) // n,
        chunks,
        chunks + (left_over[1] + (n - 1)) // n,
    ]

    p_high, p_low = split(probe_ref[...])

    def contents(t, chunk):
        values = arrived_ref[pl.ds(chunk * per, per), t * slots : (t + 1) * slots, :]
        fact = jnp.concatenate([fact_ref[t * chunks + chunk], jnp.zeros((COLS - 8, n), f32)], 0)
        return values.reshape(n, COLS), fact.T

    def moved(chosen, t, chunk):
        values, fact = contents(t, chunk)
        both = jnp.concatenate([values, fact.astype(bf16)], 1)
        return dot(chosen.astype(f32).astype(bf16), both)

    def direct(k, chunk):
        values, fact = contents(main[k], chunk)
        total = jnp.concatenate([values.astype(f32), fact], 1)
        if chunks == 1 and k != 1:
            guest = moved(fact[:, 7:8] == rank_ref[rim_tile[k]], rim_tile[k], 0)
            total = jnp.where(fact[:, 0:1] > 0.0, total, guest)
        finish(first[k] + chunk, total)

    def extra(k, q):
        wanted = iota((n, n), 0).astype(f32) + ((q - chunks) * n).astype(f32) + seated[k // 2]

        def gather(chunk, total):
            t = rim_tile[k]
            part = moved(wanted == rank_ref[t * chunks + chunk], t, chunk)
            return part if total is None else total + part

        total = None if chunks == 1 else jnp.zeros((n, 2 * COLS), f32)
        finish(first[k] + q, over(chunks, gather, total))

    def finish(b, total):
        flip = total.T
        vt_ref[b] = flip[:COLS]
        row, h = flip[COLS : COLS + 1] - 1.0, flip[COLS + 1 : COLS + 2] - 1.0
        column = total[:, COLS : COLS + 8] - 1.0
        ohm_ref[b] = (iota((ROWS, n), 0).astype(f32) == row).astype(f32).astype(bf16)
        ohmt_ref[b] = (iota((n, ROWS), 1).astype(f32) == column[:, 0:1]).astype(f32).astype(bf16)
        ohht_ref[b] = jnp.concatenate(
            [
                (iota((n, HC), 1).astype(f32) == column[:, 2 + p : 3 + p]).astype(f32)
                for p in range(3)
            ],
            1,
        ).astype(bf16)
        ohh = (iota((HC, n), 0).astype(f32) == h).astype(f32).astype(bf16)
        wt_ref[b] = dot(p_high, ohh) + dot(p_low, ohh)

    for k in range(3):

        def place(chunk, carry, k=k):
            direct(k, chunk)
            return carry

        over(chunks, place, 0)

    one_block = jnp.maximum(filled[0], filled[2]) <= 1

    @pl.when(jnp.logical_not(one_block))
    def _():
        for k in (0, 2):

            def more(q, carry, k=k):
                extra(k, q)
                return carry

            lax.fori_loop(chunks, filled[k], more, 0)

    st_ref[:, :, RANK:, :] = jnp.zeros((3, JG, RP - RANK, ROWS), f32)
    pp_ref[:, :, RANK:, :] = jnp.zeros((3, FDEV, RP - RANK, COLS), f32)
    lane = iota((RANK * JG, ROWS), 1)

    def step(g, carry, short, gram_ref, start):
        def sketch_of(b):
            w = wt_ref[b]
            u = []
            for j in range(JG):
                re = vt_ref[b, pl.ds(g * JG + j, 1), :]
                im = vt_ref[b, pl.ds(FDEV + g * JG + j, 1), :]
                u.append(w[:RANK] * re + w[RANK:] * im)
            return dot(jnp.concatenate(u, 0).astype(bf16), ohmt_ref[b])

        def project_of(b, rows):
            at = dot(rows, ohm_ref[b])
            z = []
            for c in range(2):
                for j in range(JG):
                    v = vt_ref[b, pl.ds(c * FDEV + g * JG + j, 1), :]
                    z.append(at[j * RANK : (j + 1) * RANK] * v)
            return dot(jnp.concatenate(z, 0).astype(bf16), ohht_ref[b])

        sketch = [sketch_of(first[k]) for k in range(3)]
        if not short:
            for k in range(3):
                sketch[k] = lax.fori_loop(
                    1, filled[k], lambda q, x, k=k: x + sketch_of(first[k] + q), sketch[k]
                )
        left, own, right = sketch
        sk = [x.astype(bf16) for x in sketch]
        proj = sum(project_of(first[k], sk[k]) for k in range(3))
        if not short:
            for k in range(3):
                proj = lax.fori_loop(
                    1, filled[k], lambda q, x, k=k: x + project_of(first[k] + q, sk[k]), proj
                )
        full_left = jnp.where(lane < ROWS - RIM, left, pltpu.roll(own, ROWS - RIM, 1))
        full_right = jnp.where(lane < ROWS - RIM, right, pltpu.roll(own, ROWS - OWN_ROWS, 1))
        full_own = jnp.where(
            lane < OWN_ROWS,
            own,
            jnp.where(lane < OWN_ROWS + RIM, left, pltpu.roll(right, ROWS - RIM, 1)),
        )
        half = RANK * JG
        re, im = proj[:half], proj[half:]
        lo = iota((half, COLS), 1) < HC
        parts = [
            jnp.where(lo, re[:, :COLS], pltpu.roll(im[:, :COLS], HC, 1)),
            jnp.where(lo, pltpu.roll(re[:, :COLS], HC, 1), im[:, :COLS]),
            jnp.where(
                lo,
                jnp.concatenate([re[:, COLS:], re[:, COLS:]], 1),
                jnp.concatenate([im[:, COLS:], im[:, COLS:]], 1),
            ),
        ]
        for p, whole in enumerate((full_left, full_own, full_right)):
            st_ref[p, :, :RANK, :] = whole.reshape(JG, RANK, ROWS)
            pp_ref[p, pl.ds(g * JG, JG), :RANK, :] = parts[p].reshape(JG, RANK, COLS)
            pad = st_ref[p].reshape(JG * RP, ROWS).astype(bf16)
            if p == 1:
                for q2 in range(2):
                    quad = st_ref[p, 4 * q2 : 4 * q2 + 4].reshape(4 * RP, ROWS)
                    own_ref[2 * g + q2] = quad.T
            gram = lax.dot_general(
                whole.astype(bf16), pad, (((1,), (1,)), ((), ())), preferred_element_type=f32
            )
            for q2 in range(2):
                lanes = iota((RANK, 4 * RP), 1) // RP
                acc = jnp.zeros((RANK, 4 * RP), f32)
                for q in range(4):
                    at = (q2 * 4 + q) * RANK
                    piece = gram[at : at + RANK, q2 * 4 * RP : (q2 + 1) * 4 * RP]
                    acc = jnp.where(lanes == q, piece, acc)
                gram_ref[:, p * (FDEV // 8) + 2 * (g - start) + q2, :] = acc
        return carry


    steps = FDEV // JG
    half = steps // 2

    @pl.when(one_block)
    def _():
        early = functools.partial(step, short=True, gram_ref=first_ref, start=0)
        lax.fori_loop(0, half, early, 0, unroll=UNROLL)
        work = invert(first_ref)
        for g in range(half, steps):
            for _ in range(PER_STEP):
                next(work, None)
            step(g, 0, True, second_ref, half)
        for _ in work:
            pass

    @pl.when(jnp.logical_not(one_block))
    def _():
        for i, ref in enumerate((first_ref, second_ref)):
            body = functools.partial(step, short=False, gram_ref=ref, start=i * half)
            lax.fori_loop(i * half, (i + 1) * half, body, 0)
        for _ in invert(first_ref):
            pass


def invert(gram_ref):
    wide = 4 * RP
    count = gram_ref.shape[1]
    lane = iota((count, wide), 1) % RP
    base = iota((count, wide), 1) // RP * RP
    same = (iota((wide, wide), 0) // RP == iota((wide, wide), 1) // RP).astype(f32)
    a = [gram_ref[r] for r in range(RANK)]
    diag = jnp.zeros((count, wide), f32)
    for r in range(RANK):
        diag = jnp.where(lane == r, a[r], diag)
    trace = jnp.dot(diag, same, preferred_element_type=f32, precision=lax.Precision.HIGHEST)
    ridge = 0.01 * trace / RANK + 1e-06
    a = [jnp.where(lane == r, a[r] + ridge, a[r]) for r in range(RANK)]
    for k in range(0, RANK, 2):
        c0 = [jnp.take_along_axis(x, base + k, axis=1) for x in a]
        c1 = [jnp.take_along_axis(x, base + (k + 1), axis=1) for x in a]
        x, y, z = c0[k], c1[k], c1[k + 1]
        scale = 1.0 / (x * z - y * y)
        x, y, z = z * scale, -y * scale, x * scale
        n0 = jnp.where(lane == k, x, jnp.where(lane == k + 1, y, x * a[k] + y * a[k + 1]))
        n1 = jnp.where(lane == k, y, jnp.where(lane == k + 1, z, y * a[k] + z * a[k + 1]))
        pair = lane // 2 == k // 2
        for r in range(RANK):
            if r // 2 != k // 2:
                a[r] = jnp.where(pair, 0.0, a[r]) - c0[r] * n0 - c1[r] * n1
        a[k], a[k + 1] = n0, n1
        yield
    for r in range(RANK):
        gram_ref[r] = a[r]


def write(
    tiles,
    own_ref,
    pp_ref,
    first_ref,
    second_ref,
    out_ref,
    sem,
    freq_ref,
    cells_ref,
    weights_ref,
    rim_ref,
):
    count = FDEV // 4
    wide = 4 * RP
    here = lax.axis_index("grid")
    has_left = (here > 0).astype(f32)
    has_right = (here < tiles - 1).astype(f32)
    rim = RIM // 2
    edge = iota((rim * JG, 1), 0) < MY // 2 * JG
    taper_first = jnp.where(edge, 0.6, 0.8)
    taper_last = jnp.where(edge, 0.8, 0.6)
    left_w = jnp.where(edge, 0.4, 0.2) * has_left
    right_w = jnp.where(edge, 0.2, 0.4) * has_right
    lo = iota((wide, COLS), 1) < HC
    mine = [iota((JG, wide), 1) // RP + 4 * q2 == iota((JG, wide), 0) for q2 in range(2)]

    def expand(take, pairs):
        rows = []
        for m in pairs:
            row = []
            for parity in range(2):
                for q2 in range(2):
                    row.append(jnp.where(mine[q2], take(q2, 2 * m + parity), 0.0))
            rows.append(jnp.concatenate(row, 1))
        return jnp.concatenate(rows, 0).astype(bf16)

    def own_rows(g, pairs):
        return expand(lambda q2, m: own_ref[2 * g + q2, pl.ds(m, 1), :], pairs)

    def rim_rows(g, side):
        return expand(lambda q2, m: rim_ref[g, side, q2, pl.ds(m, 1), :], range(rim))

    def weights(g, gram_ref, start):
        w = []
        for p in range(3):
            even, odd = [], []
            for q2 in range(2):
                i = 2 * g + q2
                inverse = gram_ref[:, p * (FDEV // 8) + i - 2 * start, :]
                lanes = iota((RANK, wide), 1) // RP
                zero = jnp.zeros((RP - RANK, wide), f32)
                diag = []
                for q in range(4):
                    diag += [jnp.where(lanes == q, inverse, 0.0), zero]
                b_high, b_low = split(jnp.concatenate(diag, 0))
                c = pp_ref[p, pl.ds(i * 4, 4)].reshape(wide, COLS)
                if p == 1:
                    p_high, p_low = split(c)
                    terms = jnp.concatenate(
                        [
                            jnp.concatenate([p_high, p_low], 1),
                            jnp.concatenate([p_high, jnp.zeros_like(p_low)], 1),
                        ],
                        0,
                    )
                    twice = dot(jnp.concatenate([b_high, b_low], 1), terms)
                    c = twice[:, :COLS] + twice[:, COLS:]
                else:
                    edge_rows = pl.ds(0 if p == 0 else OWN_ROWS - RIM, RIM)
                    x = own_ref[i, edge_rows, :].astype(bf16)
                    twice = dot(x, jnp.concatenate([b_high, b_low], 1))
                    rim_ref[g, p // 2, q2] = twice[:, :wide] + twice[:, wide:]
                r = pltpu.roll(c, HC, 1)
                even.append(jnp.concatenate([jnp.where(lo, c, 0.0), jnp.where(lo, r, 0.0)], 1))
                odd.append(jnp.concatenate([jnp.where(lo, 0.0, r), jnp.where(lo, 0.0, c)], 1))
            w.append(jnp.concatenate(even + odd, 0).astype(bf16))
        return w

    def put(pairs, g, full):
        for c in range(2):
            part = full[:, c * COLS : (c + 1) * COLS].reshape(len(pairs), JG, COLS)
            at = pl.ds(c * FDEV + g * JG, JG)
            freq_ref[pairs.start : pairs.stop, at, :] = part

    steps = FDEV // JG
    half = steps // 2
    work = invert(second_ref)
    blocks = PAIRS // rim
    for g in range(half):
        for _ in range(PER_STEP):
            next(work, None)
        w = weights(g, first_ref, 0)
        mid = dot(own_rows(g, range(PAIRS)), w[1])
        first, last = rim * JG, (PAIRS - rim) * JG
        begin = mid[:first] * taper_first + dot(rim_rows(g, 0), w[0]) * left_w
        end = mid[last:] * taper_last + dot(rim_rows(g, 1), w[2]) * right_w
        put(range(PAIRS), g, jnp.concatenate([begin, mid[first:last], end], 0))
    for _ in work:
        pass

    def late(g, carry):
        for p, x in enumerate(weights(g, second_ref, half)):
            weights_ref[g - half, p] = x
        return carry

    lax.fori_loop(half, steps, late, 0, unroll=4)
    copies = []
    for b in range(blocks):
        pairs = range(b * rim, (b + 1) * rim)
        for g in range(half, steps):
            part = dot(own_rows(g, pairs), weights_ref[g - half, 1])
            if b == 0:
                part = part * taper_first + dot(rim_rows(g, 0), weights_ref[g - half, 0]) * left_w
            elif b == blocks - 1:
                part = part * taper_last + dot(rim_rows(g, 1), weights_ref[g - half, 2]) * right_w
            put(pairs, g, part)
        for m in pairs:
            cells_ref[2 * m : 2 * m + 2] = freq_ref[m].T.reshape(2, HC, COLS)
        cells = pl.ds(2 * rim * b, 2 * rim)
        copy = pltpu.make_async_copy(cells_ref.at[cells], out_ref.at[cells], sem.at[b])
        copy.start()
        copies.append(copy)
    for copy in copies:
        copy.wait()


def patches(arrived, probe, tiles, slots):
    return pl.pallas_call(
        functools.partial(patch_kernel, tiles, slots),
        out_shape=jax.ShapeDtypeStruct((OWN_ROWS, HC, COLS), f32),
        in_specs=[pl.BlockSpec(memory_space=pltpu.VMEM)] * 2,
        out_specs=pl.BlockSpec(memory_space=pl.ANY),
        scratch_shapes=[
            pltpu.VMEM((3, JG, RP, ROWS), f32),
            pltpu.VMEM((3, FDEV, RP, COLS), f32),
            pltpu.VMEM((FDEV // 4, ROWS, 4 * RP), f32),
            pltpu.VMEM((RANK, 3 * FDEV // 8, 4 * RP), f32),
            pltpu.VMEM((RANK, 3 * FDEV // 8, 4 * RP), f32),
            pltpu.SemaphoreType.DMA((6,)),
        ],
        compiler_params=pltpu.CompilerParams(vmem_limit_bytes=60 * 2**20),
        name="patches",
    )(arrived, probe)


def per_device(traces, bins, live, probe):
    tiles = lax.axis_size("grid")
    bands = lax.axis_size("freq")
    slots, length = traces.shape[2:]
    sources = tiles * bands
    used = SPAN * slots

    vmem = pl.BlockSpec(memory_space=pltpu.VMEM)
    sent = pl.pallas_call(
        spectra_kernel,
        out_shape=jax.ShapeDtypeStruct((tiles, bands, used + 2, COLS), bf16),
        in_specs=[pl.BlockSpec(memory_space=pl.ANY)] * 3,
        out_specs=vmem,
        scratch_shapes=[
            pltpu.VMEM((length, COLS * bands), bf16),
            pltpu.VMEM((tiles * slots, length), bf16),
            pltpu.VMEM((tiles, slots), jnp.int32),
            pltpu.VMEM((tiles, slots), jnp.int32),
            pltpu.SemaphoreType.DMA((3,)),
        ],
        compiler_params=pltpu.CompilerParams(vmem_limit_bytes=60 * 2**20),
        name="spectra",
    )(traces.reshape(tiles * slots, length), bins[0], live[0])

    arrived = lax.all_to_all(
        sent.reshape(sources, used + 2, COLS), ("grid", "freq"), 0, 0, tiled=True
    )

    out = patches(
        arrived, jnp.transpose(probe, (1, 2, 0)).reshape(2 * RANK, HC), tiles, slots
    )
    return out.reshape(OWNX, MY, HC, COLS)


def solution(mesh):
    placed = (
        P(("grid", "freq"), None, None, None),
        P(("grid", "freq"), None, None),
        P(("grid", "freq"), None, None),
        P(),
    )
    return jax.shard_map(
        per_device,
        mesh=mesh,
        in_specs=placed,
        out_specs=P("grid", None, None, "freq"),
        check_vma=False,
    )
```
